32 devices in a mesh: slab: 2 (over y), aa: 4 (over z), ba: 4 (over x, core).
Axes of the slice: x: 2, y: 2, z: 4, core: 2. Of those that a mesh axis runs over, the one named last changes fastest.
Arguments:
- slab_field: float32 [8, 512, 512, 256], P('slab', 'aa', 'ba'), parts along dimension 0, may hold values from -18 to 18
- x_basis: float32 [1024, 128], P('slab'), parts along dimension 0, may hold values from -0.25 to 0.25
- y_basis: float32 [1024, 128], P('slab'), parts along dimension 0, may hold values from -0.25 to 0.25
Outputs:
- new_basis: float32 [1024, 128], P(('slab', 'aa')), parts along dimension 0
- core_tensor: float32 [8, 128, 128, 256], P('slab', None, 'aa', 'ba'), parts along dimension 0
The draws below stay inside these ranges and needn't reach their ends.
There are 2 independent parts, one for each index of `slab`. The reference program is written for one: setup_inputs(seed, part) draws one part's arguments, and reference() takes and returns one part's arrays. A program takes and returns all parts, laid end to end along the dimension named above; each array names one. Nothing has to cross between parts.
All inputs are finite; a program needn't handle non-finite values.
Results may differ from the reference program's by a relative error of at most 0.00023.
Values sent between devices are 32-bit elements; how exact they have to be, the bound alone decides.
No kernel may reach another device: no remote copies, remote signals or barrier semaphores. Data moves between devices by JAX's collectives and lax.ppermute only.
A program may use at most 384 MiB of HBM per device.

```python
import math
import jax
import jax.numpy as jnp
from jax import lax

S = 4
NX = 512
NY = 512
R = 128
NZ = 256
ITERS = 2


def draw_slab_field(key, part):
    key = jax.random.fold_in(key, 7)
    key_base, key_rows = jax.random.split(key, 2)
    row_scale = jnp.exp(jax.random.uniform(key_rows, (1, NX, 1, 1), jnp.float32, 0.0, math.log(3.0)))
    base = jnp.clip(jax.random.normal(key_base, (S, NX, NY, NZ), jnp.float32), -6.0, 6.0)
    return base * row_scale


def gaussian(own_key, extent, deviation, most, dtype=jnp.bfloat16):
    return jnp.clip(deviation * jax.random.normal(own_key, extent, jnp.float32), -most, most).astype(dtype)


def setup_inputs(seed: int = 0, part: int = 0) -> dict:
    arg_keys = jax.random.split(jax.random.key(seed), 4)
    part_splits = jax.random.split(jax.random.fold_in(arg_keys[3], part), 4)
    return {
        "slab_field": draw_slab_field(jax.random.fold_in(jax.random.fold_in(arg_keys[3], part), 71), part),
        "x_basis": gaussian(part_splits[1], (NX, R), NX ** -0.5, 0.25, jnp.float32),
        "y_basis": gaussian(part_splits[2], (NY, R), NY ** -0.5, 0.25, jnp.float32),
    }


def orthonormal(images):
    small = jnp.dot(images.T, images, precision=lax.Precision.HIGHEST)
    lower = jnp.linalg.cholesky(small)
    return lax.linalg.triangular_solve(lower, images, left_side=False, lower=True, transpose_a=True)

def reference(slab_field, x_basis, y_basis):
    highest = lax.Precision.HIGHEST
    projected = jnp.einsum('sxyz,yr->sxrz', slab_field, y_basis, precision=highest)
    gram_matrix = jnp.einsum('sxrz,svrz->xv', projected, projected, precision=highest)
    basis = x_basis
    for step in range(ITERS):
        images = jnp.dot(gram_matrix, basis, precision=highest)
        basis = orthonormal(images)
    core_tensor = jnp.einsum('xk,sxrz->skrz', basis, projected, precision=highest)
    return (basis, core_tensor)
```

```python
import jax
import jax.numpy as jnp
from jax import lax
from jax.experimental import pallas as pl
from jax.experimental.pallas import tpu as pltpu
from jax.sharding import PartitionSpec as P

ITERS = 2
F32 = jnp.float32
BF16 = jnp.bfloat16
HIGHEST = lax.Precision.HIGHEST
MIB = 1 << 20
X_PARTS = 4
R_PARTS = 4
LANES = 128
PAIRS = ((0, 0), (1, 0), (1, 1))


def split(value):
    high = value.astype(BF16)
    return high, (value - high.astype(F32)).astype(BF16)


def nt_dot(left, right):
    return lax.dot_general(left, right, (((1,), (1,)), ((), ())), preferred_element_type=F32)


def tn_dot(left, right):
    return lax.dot_general(left, right, (((0,), (0,)), ((), ())), preferred_element_type=F32)


def call(kernel, grid, in_specs, out_specs, out_shape, scratch=(), vmem=48, flops=0, moved=0):
    return pl.pallas_call(
        kernel,
        grid_spec=pltpu.PrefetchScalarGridSpec(
            num_scalar_prefetch=1, grid=grid, in_specs=in_specs, out_specs=out_specs, scratch_shapes=list(scratch)
        ),
        out_shape=out_shape,
        compiler_params=pltpu.CompilerParams(vmem_limit_bytes=vmem * MIB, dimension_semantics=("arbitrary",) * len(grid)),
        cost_estimate=pl.CostEstimate(flops=flops, bytes_accessed=moved, transcendentals=0),
    )


def project_kernel(parts, place, own_ref, other_ref, basis_ref, *rest):
    outs, basis_split = rest[:-1], rest[-1]
    keeps, sends = outs[:parts], outs[parts:]
    rank = basis_ref.shape[0]

    @pl.when(pl.program_id(0) == 0)
    def _():
        high, low = split(basis_ref[...])
        basis_split[0:rank, :] = high
        basis_split[rank:, :] = low

    first = place[0] == 0
    stacked = basis_split[...]
    for i in range(own_ref.shape[1]):
        high, low = split(jnp.concatenate([own_ref[0, i], other_ref[i]], axis=0))
        both = jnp.dot(stacked, high, preferred_element_type=F32)
        out = both[:rank] + (both[rank:] + jnp.dot(stacked[:rank], low, preferred_element_type=F32))
        left, right = out[:, :LANES], out[:, LANES:]
        keep, send = jnp.where(first, left, right), jnp.where(first, right, left)
        rows = rank // 4 // parts
        for a in range(4):
            for part in range(parts):
                at = (a * parts + part) * rows
                keeps[part][a, :, i, :] = keep[at : at + rows]
                sends[part][a, :, i, :] = send[at : at + rows]


def project(place, field, other, basis, species, x_start, parts):
    xs, ys, zs = other.shape
    rank = basis.shape[0]
    block = 8
    shape = (4, rank // 4 // parts, xs, zs // 2)
    out = pl.BlockSpec((4, shape[1], block, shape[3]), lambda i, place: (0, 0, i, 0))
    kernel = lambda place, *refs: project_kernel(parts, place, *refs)
    result = call(
        kernel,
        (xs // block,),
        [
            pl.BlockSpec((1, block, ys, zs), lambda i, place: (2 * place[1] + species, x_start // block + i, 0, 0)),
            pl.BlockSpec((block, ys, zs), lambda i, place: (i, 0, 0)),
            pl.BlockSpec(basis.shape, lambda i, place: (0, 0)),
        ],
        [out] * (2 * parts),
        [jax.ShapeDtypeStruct(shape, F32)] * (2 * parts),
        [pltpu.VMEM((2 * rank, 2 * ys), BF16)],
        flops=6 * xs * rank * 2 * ys * zs,
        moved=4 * xs * zs * (2 * ys + rank),
    )(place, field, other, basis)
    return result[:parts], result[parts:]


def add_kernel(place, keep_ref, recv_ref, *outs):
    for d in range(4):
        to = lax.rem(place[2] + d, 4)
        outs[d][...] = keep_ref[to] + recv_ref[to]


def add_up(place, keep, recv):
    _, rows, xs, zs = keep.shape
    block = max(1, 4 * LANES // xs)
    spec = pl.BlockSpec((4, block, xs, zs), lambda i, place: (0, i, 0, 0))
    out = pl.BlockSpec((block, xs, zs), lambda i, place: (i, 0, 0))
    return call(
        add_kernel,
        (rows // block,),
        [spec, spec],
        [out] * 4,
        [jax.ShapeDtypeStruct((rows, xs, zs), F32)] * 4,
        moved=12 * keep.size,
    )(place, keep, recv)


def gram_kernel(parts, place, start_ref, *rest):
    lines, (out_ref, high_ref, low_ref) = rest[: 4 * parts], rest[4 * parts :]
    rows, xs = lines[0].shape[:2]

    @pl.when(pl.program_id(0) == 0)
    def _():
        out_ref[...] = start_ref[...]

    for d in range(4):
        base = pl.multiple_of(lax.rem(place[2] + 4 - d, 4) * (parts * xs), parts * xs)
        for r in range(rows):
            block = jnp.concatenate([lines[d * parts + p][r] for p in range(parts)], axis=0)
            high, low = split(block)
            high_ref[pl.ds(base, parts * xs), r * LANES : (r + 1) * LANES] = high
            low_ref[pl.ds(base, parts * xs), r * LANES : (r + 1) * LANES] = low
    size = out_ref.shape[1]
    for index, (i, j) in enumerate(PAIRS):
        hi, li = high_ref[i * size : (i + 1) * size], low_ref[i * size : (i + 1) * size]
        hj, lj = high_ref[j * size : (j + 1) * size], low_ref[j * size : (j + 1) * size]
        out_ref[index * size : (index + 1) * size, :] += nt_dot(hi, hj) + (nt_dot(hi, lj) + nt_dot(li, hj))


def add_gram(place, start, lines):
    parts = len(lines[0])
    rows, xs, zs = lines[0][0].shape
    block = 8
    total = 4 * parts * xs
    line = pl.BlockSpec((block, xs, zs), lambda i, place: (i, 0, 0))
    whole = pl.BlockSpec(start.shape, lambda i, place: (0, 0))
    return call(
        lambda place, *refs: gram_kernel(parts, place, *refs),
        (rows // block,),
        [whole] + [line] * (4 * parts),
        whole,
        jax.ShapeDtypeStruct(start.shape, F32),
        [pltpu.VMEM((total, block * zs), BF16)] * 2,
        flops=6 * start.size * rows * zs,
        moved=4 * total * rows * zs,
    )(place, start, *[piece for group in lines for piece in group])


def inverse_factor(small):
    n = small.shape[0]
    rows = lax.broadcasted_iota(jnp.int32, (n, n), 0)
    cols = lax.broadcasted_iota(jnp.int32, (n, n), 1)
    unit = jnp.where(rows == cols, 1.0, 0.0).astype(F32)
    tiles = [small[8 * t : 8 * t + 8] for t in range(n // 8)]
    units = [unit[8 * t : 8 * t + 8] for t in range(n // 8)]
    sub = lax.broadcasted_iota(jnp.int32, (8, n), 0)
    done = [None] * (n // 8)
    for j in range(n):
        at, r = divmod(j, 8)
        row, unit_row = tiles[at][r : r + 1], units[at][r : r + 1]
        pivot = row[:, j : j + 1]
        inverse = 1.0 / pivot
        scale = lax.rsqrt(pivot)
        scaled = row * inverse
        for t in range(at, n // 8):
            column = tiles[t][:, j : j + 1]
            if t == at:
                column = jnp.where(sub[:, 0:1] > r, column, 0.0)
            factor = column * inverse
            tiles[t] = tiles[t] - factor * row
            units[t] = units[t] - factor * unit_row
        piece = jnp.where(sub == r, unit_row * scale, 0.0)
        done[at] = piece if r == 0 else done[at] + piece
    return jnp.concatenate(done, axis=0)


def basis_kernel(place, pieces_ref, start_ref, out_ref, gram_ref):
    count, size = pieces_ref.shape[0], pieces_ref.shape[1]
    for core in range(2):
        for chip in range(2):
            for d in range(4):
                at = (
                    lax.rem(place[1] + core, 2) * 8
                    + lax.rem(place[0] + chip, 2) * 4
                    + lax.rem(place[2] + 4 - d, 4)
                )
                gram_ref[pl.ds(pl.multiple_of(at * size, 8), size), :] = pieces_ref[(core * 2 + chip) * 4 + d]
    half = gram_ref.shape[1]
    g00, g10, g11 = (gram_ref[i * half : (i + 1) * half, :] for i in range(3))
    g01 = g10.T
    basis = start_ref[...]
    for _ in range(ITERS):
        top, low = basis[:half], basis[half:]
        dot = lambda a, b: jnp.dot(a, b, precision=HIGHEST, preferred_element_type=F32)
        images = jnp.concatenate([dot(g00, top) + dot(g01, low), dot(g10, top) + dot(g11, low)], axis=0)
        small = dot(images.T, images)
        basis = dot(images, inverse_factor(small).T)
    out_ref[...] = basis


def subspace(place, pieces, start):
    count, size, width = pieces.shape
    return call(
        basis_kernel,
        (1,),
        [
            pl.BlockSpec(pieces.shape, lambda i, place: (0, 0, 0)),
            pl.BlockSpec(start.shape, lambda i, place: (0, 0)),
        ],
        pl.BlockSpec(start.shape, lambda i, place: (0, 0)),
        jax.ShapeDtypeStruct(start.shape, F32),
        [pltpu.VMEM((count * size, width), F32)],
    )(place, pieces, start)


def core_kernel(parts, r_parts, place, basis_ref, *rest):
    lines, (keep_ref, send_ref, factor_ref) = rest[:-3], rest[-3:]
    rank = basis_ref.shape[1]
    xs = basis_ref.shape[0] // 4

    @pl.when(pl.program_id(0) == 0)
    def _():
        for d in range(4):
            base = pl.multiple_of(lax.rem(place[2] + 4 - d, 4) * xs, xs)
            high, low = split(basis_ref[pl.ds(base, xs), :])
            factor_ref[d * xs : (d + 1) * xs, 0:rank] = high
            factor_ref[d * xs : (d + 1) * xs, rank:] = low

    factor = factor_ref[...]

    def work(pieces):
        rows, _, zs = pieces[0].shape
        lines = [jnp.concatenate([piece[r] for piece in pieces], axis=0) for r in range(rows)]
        high, low = split(jnp.concatenate(lines, axis=1))
        both = tn_dot(high, factor)
        out = both[:, :rank] + (both[:, rank:] + tn_dot(low, factor[:, :rank]))
        out = out.reshape(rows, 2, zs // 2, rank)
        first = place[1] == 0
        keep_ref[...] = jnp.where(first, out[:, 0], out[:, 1])
        send_ref[...] = jnp.where(first, out[:, 1], out[:, 0])

    if r_parts == 1:
        work(lines)
    else:
        for part in range(r_parts):

            @pl.when(pl.program_id(0) == part)
            def _(part=part):
                work(lines[4 * part : 4 * part + 4])


def core_of(place, basis, lines, r_parts):
    parts = len(lines[0][0])
    rows, xs, zs = lines[0][0][0].shape
    block = 8
    rank = basis.shape[1]
    flat = [piece for group in lines for d in group for piece in d]
    total = rows * r_parts
    return call(
        lambda place, *refs: core_kernel(parts, r_parts, place, *refs),
        (total // block,),
        [pl.BlockSpec(basis.shape, lambda i, place: (0, 0))]
        + [pl.BlockSpec((block, xs, zs), (lambda i, place: (i, 0, 0)) if r_parts == 1 else (lambda i, place: (0, 0, 0)))]
        * len(flat),
        [pl.BlockSpec((block, zs // 2, rank), lambda i, place: (i, 0, 0))] * 2,
        [jax.ShapeDtypeStruct((total, zs // 2, rank), F32)] * 2,
        [pltpu.VMEM((basis.shape[0], 2 * rank), BF16)],
        flops=6 * basis.size * total * zs,
        moved=4 * total * zs * (basis.shape[0] + rank),
    )(place, basis, *flat)


def after(value, *earlier):
    return lax.optimization_barrier((value, *earlier))[0]


def pair_swap(value, distance):
    return lax.ppermute(value, "ba", [(i, i ^ distance) for i in range(4)])


def z_shift(value, d):
    return lax.ppermute(value, "aa", [(i, (i + d) % 4) for i in range(4)])


def reduce_gram(place, gram):
    chip, core, z = place[0], place[1], place[2]
    rows, width = gram.shape
    halves = gram.reshape(2, rows // 2, width)
    take = lambda array, i: lax.dynamic_index_in_dim(array, i, 0, keepdims=False)
    gram = take(halves, core) + pair_swap(take(halves, 1 - core), 1)
    halves = gram.reshape(2, rows // 4, width)
    gram = take(halves, chip) + pair_swap(take(halves, 1 - chip), 2)
    blocks = gram.reshape(4, rows // 16, width)
    came = [z_shift(take(blocks, (z + d) % 4), d) for d in (1, 2, 3)]
    gram = take(blocks, z) + came[0] + came[1] + came[2]
    gram = jnp.stack([gram] + [z_shift(gram, d) for d in (1, 2, 3)])
    gram = jnp.concatenate([gram, pair_swap(gram, 2)])
    return jnp.concatenate([gram, pair_swap(gram, 1)])


def fast_body(slab_field, x_basis, y_basis):
    rank = x_basis.shape[1]
    species, xs, ys, zs = slab_field.shape
    ba = lax.axis_index("ba")
    chip, core, z = ba // 2, ba % 2, lax.axis_index("aa")
    place = jnp.stack([chip, core, z]).astype(jnp.int32)
    rows = lambda index: lax.dynamic_slice_in_dim(y_basis, index * ys, ys, 0)
    basis_t = jnp.concatenate([rows(ba), rows(ba ^ 1)], axis=0).T

    def swap_field(s, start, size, *earlier):
        theirs = lax.dynamic_slice(slab_field, (2 * (1 - core) + s, start, 0, 0), (1, size, ys, zs))
        return pair_swap(after(theirs[0], *earlier), 1)

    def spread(keep, recv):
        mine = add_up(place, keep, recv)
        return [mine[0]] + [z_shift(mine[d], d) for d in (1, 2, 3)]

    keeps, sends = [], []
    step = xs // X_PARTS
    others = []
    for i in range(X_PARTS):
        others.append(swap_field(0, i * step, step, *others[-2:-1]))
    others.append(swap_field(1, 0, xs, others[-1]))
    for i in range(X_PARTS):
        keep, send = project(place, slab_field, others[i], basis_t, 0, i * step, 1)
        keeps += keep
        sends += send
    keep, send = project(place, slab_field, others[-1], basis_t, 1, 0, R_PARTS)
    keeps += keep
    sends += send

    came, lines = [], []
    for i, (keep, send) in enumerate(zip(keeps, sends)):
        if i >= 2:
            send = after(send, came[i - 2], *(lines[i - 3][1:] if i >= 3 else ()))
        came.append(pair_swap(send, 2))
        if i >= 1:
            lines.append(spread(keeps[i - 1], came[i - 1]))
    lines.append(spread(keeps[-1], came[-1]))

    gram = jnp.zeros((len(PAIRS) * xs * 2, xs * 2), F32)
    first = [[lines[p][d] for p in range(X_PARTS)] for d in range(4)]
    second = [[[lines[X_PARTS + p][d]] for d in range(4)] for p in range(R_PARTS)]
    gram = add_gram(place, gram, first)
    for group in second:
        gram = add_gram(place, gram, group)
    basis = subspace(place, reduce_gram(place, gram), x_basis)

    keep0, send0 = core_of(place, basis, [first], 1)
    came0 = pair_swap(send0, 1)
    keep1, send1 = core_of(place, basis, second, R_PARTS)
    came1 = pair_swap(send1, 1)
    mine, theirs = (keep0, keep1), (came0, came1)
    core_tensor = jnp.stack(
        [jnp.where(core == i // 2, mine[i % 2], theirs[i % 2]) for i in range(species)]
    ).transpose(0, 3, 1, 2)
    new_basis = lax.dynamic_slice_in_dim(basis, z * xs, xs, 0)
    return new_basis, core_tensor


def orthonormal(images):
    small = jnp.dot(images.T, images, precision=HIGHEST)
    lower = jnp.linalg.cholesky(small)
    return lax.linalg.triangular_solve(lower, images, left_side=False, lower=True, transpose_a=True)


def plain_body(slab_field, x_basis, y_basis):
    y_rows = slab_field.shape[2]
    local_basis = lax.dynamic_slice_in_dim(y_basis, lax.axis_index("ba") * y_rows, y_rows, 0)
    partial_value = jnp.einsum("sxyz,yr->sxrz", slab_field, local_basis, precision=HIGHEST)
    projected = lax.psum_scatter(partial_value, "ba", scatter_dimension=3, tiled=True)
    columns = lax.all_to_all(projected, "aa", split_axis=2, concat_axis=1, tiled=True)
    basis = x_basis
    local_gram = jnp.einsum("sxrz,svrz->xv", columns, columns, precision=HIGHEST)
    gram_matrix = lax.psum(local_gram, ("aa", "ba"))
    for _ in range(ITERS):
        basis = orthonormal(jnp.dot(gram_matrix, basis, precision=HIGHEST))
    core_tensor = jnp.einsum("xk,sxrz->skrz", basis, columns, precision=HIGHEST)
    basis_rows = x_basis.shape[0] // lax.axis_size("aa")
    new_basis = lax.dynamic_slice_in_dim(basis, lax.axis_index("aa") * basis_rows, basis_rows, 0)
    return new_basis, core_tensor


def solution(mesh):
    def body(slab_field, x_basis, y_basis):
        fits = (
            mesh.shape["aa"] == 4
            and mesh.shape["ba"] == 4
            and slab_field.shape == (4, LANES, LANES, 2 * LANES)
            and x_basis.shape == y_basis.shape == (4 * LANES, LANES)
        )
        return (fast_body if fits else plain_body)(slab_field, x_basis, y_basis)

    return jax.shard_map(
        body,
        mesh=mesh,
        in_specs=(P("slab", "aa", "ba", None), P("slab", None), P("slab", None)),
        out_specs=(P(("slab", "aa"), None), P("slab", None, "aa", "ba")),
        check_vma=False,
    )
```

```python
import jax
import jax.numpy as jnp
from jax import lax
from jax.experimental import pallas as pl
from jax.experimental.pallas import tpu as pltpu
from jax.sharding import PartitionSpec as P

ITERS = 2
F32 = jnp.float32
BF16 = jnp.bfloat16
HIGHEST = lax.Precision.HIGHEST
MIB = 1 << 20
X_PARTS = (16,) * 8
R_PARTS = (4,) * 8
LANES = 128
PAIRS = ((0, 0), (1, 0), (1, 1))


def split(value):
    high = value.astype(BF16)
    return high, (value - high.astype(F32)).astype(BF16)


def nt_dot(left, right):
    return lax.dot_general(left, right, (((1,), (1,)), ((), ())), preferred_element_type=F32)


def tn_dot(left, right):
    return lax.dot_general(left, right, (((0,), (0,)), ((), ())), preferred_element_type=F32)


def call(name, kernel, grid, in_specs, out_specs, out_shape, scratch=(), vmem=16):
    return pl.pallas_call(
        kernel,
        name=name,
        grid_spec=pltpu.PrefetchScalarGridSpec(
            num_scalar_prefetch=1, grid=grid, in_specs=in_specs, out_specs=out_specs, scratch_shapes=list(scratch)
        ),
        out_shape=out_shape,
        compiler_params=pltpu.CompilerParams(vmem_limit_bytes=vmem * MIB, dimension_semantics=("arbitrary",) * len(grid)),
        cost_estimate=pl.CostEstimate(flops=0, bytes_accessed=0, transcendentals=0),
    )


def project_kernel(parts, place, own_ref, other_ref, basis_ref, *rest):
    outs, basis_split = rest[:-1], rest[-1]
    keeps, sends = outs[: len(parts)], outs[len(parts) :]
    rank = basis_ref.shape[0]

    @pl.when(pl.program_id(0) == 0)
    def _():
        high, low = split(basis_ref[...])
        basis_split[0:rank, :] = high
        basis_split[rank:, :] = low

    first = place[0] == 0
    stacked = basis_split[...]
    for i in range(own_ref.shape[1]):
        high, low = split(jnp.concatenate([own_ref[0, i], other_ref[i]], axis=0))
        both = jnp.dot(stacked, high, preferred_element_type=F32)
        out = both[:rank] + (both[rank:] + jnp.dot(stacked[:rank], low, preferred_element_type=F32))
        left, right = out[:, :LANES], out[:, LANES:]
        keep, send = jnp.where(first, left, right), jnp.where(first, right, left)
        at = 0
        for a in range(4):
            for part, rows in enumerate(parts):
                keeps[part][a, :, i, :] = keep[at : at + rows]
                sends[part][a, :, i, :] = send[at : at + rows]
                at += rows


def project(place, field, other, basis, job, offset):
    species, x_start, xs, parts = job
    _, ys, zs = other.shape
    rank = basis.shape[0]
    block = 8
    steps = xs // block
    shapes = [(4, rows, xs, zs // 2) for rows in parts] * 2
    in_specs = [
        pl.BlockSpec((1, block, ys, zs), lambda i, place: (2 * place[1] + species, x_start // block + i, 0, 0)),
        pl.BlockSpec((block, ys, zs), lambda i, place: (offset // block + i, 0, 0)),
        pl.BlockSpec(basis.shape, lambda i, place: (0, 0)),
    ]
    out_specs = [pl.BlockSpec((4, s[1], block, s[3]), lambda i, place: (0, 0, i, 0)) for s in shapes]
    result = call(
        "project_k",
        lambda place, *refs: project_kernel(parts, place, *refs),
        (steps,),
        in_specs,
        out_specs,
        [jax.ShapeDtypeStruct(s, F32) for s in shapes],
        [pltpu.VMEM((2 * rank, 2 * ys), BF16)],
        vmem=18,
    )(place, field, other, basis)
    count = len(parts)
    return result[:count], result[count:]


def add_kernel(place, keep_ref, recv_ref, *outs):
    for d in range(4):
        to = lax.bitwise_xor(place[2], d)
        outs[d][...] = keep_ref[to] + recv_ref[to]


def add_up(place, keep, recv):
    _, rows, xs, zs = keep.shape
    block = min(rows, max(1, 4 * LANES // xs))
    while rows % block:
        block -= 1
    spec = pl.BlockSpec((4, block, xs, zs), lambda i, place: (0, i, 0, 0))
    out = pl.BlockSpec((block, xs, zs), lambda i, place: (i, 0, 0))
    return call(
        "add_k",
        add_kernel,
        (rows // block,),
        [spec, spec],
        [out] * 4,
        [jax.ShapeDtypeStruct((rows, xs, zs), F32)] * 4,
        vmem=12,
    )(place, keep, recv)


def gram_kernel(parts, place, start_ref, *rest):
    lines, (out_ref, high_ref, low_ref) = rest[: 4 * parts], rest[4 * parts :]
    rows = lines[0].shape[0]
    xs = high_ref.shape[0] // 4

    @pl.when(pl.program_id(0) == 0)
    def _():
        out_ref[...] = start_ref[...]

    for d in range(4):
        base = pl.multiple_of(lax.bitwise_xor(place[2], d) * xs, xs)
        for r in range(rows):
            block = jnp.concatenate([lines[d * parts + p][r] for p in range(parts)], axis=0)
            high, low = split(block)
            high_ref[pl.ds(base, xs), r * LANES : (r + 1) * LANES] = high
            low_ref[pl.ds(base, xs), r * LANES : (r + 1) * LANES] = low
    size = out_ref.shape[1]
    for index, (i, j) in enumerate(PAIRS):
        hi, li = high_ref[i * size : (i + 1) * size], low_ref[i * size : (i + 1) * size]
        hj, lj = high_ref[j * size : (j + 1) * size], low_ref[j * size : (j + 1) * size]
        out_ref[index * size : (index + 1) * size, :] += nt_dot(hi, hj) + (nt_dot(hi, lj) + nt_dot(li, hj))


def add_gram(place, start, lines):
    parts = len(lines[0])
    rows, _, zs = lines[0][0].shape
    block = min(8, rows)
    total = 2 * start.shape[1]
    flat = [piece for group in lines for piece in group]
    whole = pl.BlockSpec(start.shape, lambda i, place: (0, 0))
    return call(
        "gram_k",
        lambda place, *refs: gram_kernel(parts, place, *refs),
        (rows // block,),
        [whole] + [pl.BlockSpec((block, *piece.shape[1:]), lambda i, place: (i, 0, 0)) for piece in flat],
        whole,
        jax.ShapeDtypeStruct(start.shape, F32),
        [pltpu.VMEM((total, block * zs), BF16)] * 2,
        vmem=20,
    )(place, start, *flat)


def inverse_factor(small):
    n = small.shape[0]
    rows = lax.broadcasted_iota(jnp.int32, (n, n), 0)
    cols = lax.broadcasted_iota(jnp.int32, (n, n), 1)
    unit = jnp.where(rows == cols, 1.0, 0.0).astype(F32)
    tiles = [small[8 * t : 8 * t + 8] for t in range(n // 8)]
    units = [unit[8 * t : 8 * t + 8] for t in range(n // 8)]
    sub = lax.broadcasted_iota(jnp.int32, (8, n), 0)
    done = [None] * (n // 8)
    for j in range(n):
        at, r = divmod(j, 8)
        row, unit_row = tiles[at][r : r + 1], units[at][r : r + 1]
        pivot = row[:, j : j + 1]
        inverse = 1.0 / pivot
        scale = lax.rsqrt(pivot)
        scaled = row * inverse
        for t in range(at, n // 8):
            column = tiles[t][:, j : j + 1]
            if t == at:
                column = jnp.where(sub[:, 0:1] > r, column, 0.0)
            factor = column * inverse
            tiles[t] = tiles[t] - factor * row
            units[t] = units[t] - factor * unit_row
        piece = jnp.where(sub == r, unit_row * scale, 0.0)
        done[at] = piece if r == 0 else done[at] + piece
    return jnp.concatenate(done, axis=0)


def basis_kernel(place, pieces_ref, start_ref, out_ref, gram_ref):
    count, size = pieces_ref.shape[0], pieces_ref.shape[1]
    for core in range(2):
        for chip in range(2):
            for d in range(4):
                at = (
                    lax.rem(place[1] + core, 2) * 8
                    + lax.rem(place[0] + chip, 2) * 4
                    + lax.bitwise_xor(place[2], d)
                )
                gram_ref[pl.ds(pl.multiple_of(at * size, 8), size), :] = pieces_ref[(core * 2 + chip) * 4 + d]
    half = gram_ref.shape[1]
    g00, g10, g11 = (gram_ref[i * half : (i + 1) * half, :] for i in range(3))
    g01 = g10.T
    basis = start_ref[...]
    for _ in range(ITERS):
        top, low = basis[:half], basis[half:]
        dot = lambda a, b: jnp.dot(a, b, precision=HIGHEST, preferred_element_type=F32)
        images = jnp.concatenate([dot(g00, top) + dot(g01, low), dot(g10, top) + dot(g11, low)], axis=0)
        small = dot(images.T, images)
        basis = dot(images, inverse_factor(small).T)
    out_ref[...] = basis


def subspace(place, pieces, start):
    count, size, width = pieces.shape
    return call(
        "subspace_k",
        basis_kernel,
        (1,),
        [
            pl.BlockSpec(pieces.shape, lambda i, place: (0, 0, 0)),
            pl.BlockSpec(start.shape, lambda i, place: (0, 0)),
        ],
        pl.BlockSpec(start.shape, lambda i, place: (0, 0)),
        jax.ShapeDtypeStruct(start.shape, F32),
        [pltpu.VMEM((count * size, width), F32)],
        vmem=12,
    )(place, pieces, start)


def core_kernel(counts, steps, place, basis_ref, *rest):
    lines, (keep_ref, send_ref, factor_ref) = rest[:-3], rest[-3:]
    rank = basis_ref.shape[1]
    xs = basis_ref.shape[0] // 4

    @pl.when(pl.program_id(0) == 0)
    def _():
        for d in range(4):
            base = pl.multiple_of(lax.bitwise_xor(place[2], d) * xs, xs)
            high, low = split(basis_ref[pl.ds(base, xs), :])
            factor_ref[d * xs : (d + 1) * xs, 0:rank] = high
            factor_ref[d * xs : (d + 1) * xs, rank:] = low

    factor = factor_ref[...]

    def work(groups):
        lines = [
            jnp.concatenate([piece[r] for piece in pieces], axis=0) for pieces in groups for r in range(pieces[0].shape[0])
        ]
        high, low = split(jnp.concatenate(lines, axis=1))
        both = tn_dot(high, factor)
        out = both[:, :rank] + (both[:, rank:] + tn_dot(low, factor[:, :rank]))
        out = out.reshape(len(lines), 2, LANES // 2, rank)
        first = place[1] == 0
        keep_ref[...] = jnp.where(first, out[:, 0], out[:, 1])
        send_ref[...] = jnp.where(first, out[:, 1], out[:, 0])

    groups, at = [], 0
    for count in counts:
        groups.append(lines[at : at + count])
        at += count
    if steps is None:
        work(groups)
    else:
        for step, members in enumerate(steps):

            @pl.when(pl.program_id(0) == step)
            def _(members=members):
                work([groups[member] for member in members])


def core_of(place, basis, lines):
    block = 8
    rank = basis.shape[1]
    groups = [[piece for d in group for piece in d] for group in lines]
    flat = [piece for group in groups for piece in group]
    rows = [group[0].shape[0] for group in groups]
    total, zs = sum(rows), flat[0].shape[2]
    if len(groups) == 1:
        steps = None
        specs = [pl.BlockSpec((block, *piece.shape[1:]), lambda i, place: (i, 0, 0)) for piece in flat]
    else:
        steps, at = [[] for _ in range(total // block)], 0
        for member, count in enumerate(rows):
            steps[at // block].append(member)
            at += count
        specs = [pl.BlockSpec(piece.shape, lambda i, place: (0, 0, 0)) for piece in flat]
    return call(
        "core_k",
        lambda place, *refs: core_kernel([len(group) for group in groups], steps, place, *refs),
        (total // block,),
        [pl.BlockSpec(basis.shape, lambda i, place: (0, 0))] + specs,
        [pl.BlockSpec((block, zs // 2, rank), lambda i, place: (i, 0, 0))] * 2,
        [jax.ShapeDtypeStruct((total, zs // 2, rank), F32)] * 2,
        [pltpu.VMEM((basis.shape[0], 2 * rank), BF16)],
        vmem=36,
    )(place, basis, *flat)


def after(value, *earlier):
    return lax.optimization_barrier((value, *earlier))[0]


def pair_swap(value, distance):
    return lax.ppermute(value, "ba", [(i, i ^ distance) for i in range(4)])


def z_swap(value, d):
    return lax.ppermute(value, "aa", [(i, i ^ d) for i in range(4)])


def reduce_gram(place, gram):
    chip, core, z = place[0], place[1], place[2]
    rows, width = gram.shape
    halves = gram.reshape(2, rows // 2, width)
    take = lambda array, i: lax.dynamic_index_in_dim(array, i, 0, keepdims=False)
    gram = take(halves, core) + pair_swap(take(halves, 1 - core), 1)
    halves = gram.reshape(2, rows // 4, width)
    gram = take(halves, chip) + pair_swap(take(halves, 1 - chip), 2)
    blocks = gram.reshape(4, rows // 16, width)
    came = [z_swap(take(blocks, z ^ d), d) for d in (1, 2, 3)]
    gram = take(blocks, z) + came[0] + came[1] + came[2]
    gram = jnp.stack([gram] + [z_swap(gram, d) for d in (1, 2, 3)])
    gram = jnp.concatenate([gram, pair_swap(gram, 2)])
    return jnp.concatenate([gram, pair_swap(gram, 1)])


def fast_body(slab_field, x_basis, y_basis):
    rank = x_basis.shape[1]
    species, xs, ys, zs = slab_field.shape
    ba = lax.axis_index("ba")
    chip, core, z = ba // 2, ba % 2, lax.axis_index("aa")
    place = jnp.stack([chip, core, z]).astype(jnp.int32)
    rows = lambda index: lax.dynamic_slice_in_dim(y_basis, index * ys, ys, 0)
    basis_t = jnp.concatenate([rows(ba), rows(ba ^ 1)], axis=0).T

    share = rank // 4
    jobs, at = [], 0
    for size in X_PARTS:
        jobs.append((0, at, size, (share,)))
        at += size
    jobs.append((1, 0, xs, R_PARTS))
    keeps, sends, came, lines = [], [], [], []

    def spread(i):
        mine = add_up(place, keeps[i], came[i])
        line = [mine[0], None, None, None]
        for d, earlier in ((2, 1), (3, 2), (1, 3)):
            part = after(mine[d], lines[-1][earlier]) if lines else mine[d]
            line[d] = z_swap(part, d)
        lines.append(line)

    def exchange(part):
        i = len(came)
        earlier = came[i - 2 : i - 1] + (lines[i - 3][1:] if i >= 3 else []) if i >= 2 else []
        came.append(pair_swap(after(part, *earlier), 2))
        if i >= 1:
            spread(i - 1)

    swaps = [(0, 0, X_PARTS[0]), (0, X_PARTS[0], xs - X_PARTS[0]), (1, 0, xs)]
    others, theirs = [], []
    for job in jobs:
        while swaps and swaps[0][:2] <= job[:2]:
            s, start, size = swaps.pop(0)
            earlier = ([], sends[:1], theirs[-1:])[len(theirs)]
            first = after(2 * (1 - core) + s, *earlier)
            theirs.append(lax.dynamic_slice(slab_field, (first, start, 0, 0), (1, size, ys, zs))[0])
            others.append((start, pair_swap(theirs[-1], 1)))
        base, other = others[-1]
        keep, send = project(place, slab_field, other, basis_t, job, job[1] - base)
        for mine, part in zip(keep, send):
            keeps.append(mine)
            sends.append(part)
            exchange(part)
    spread(len(keeps) - 1)

    gram = jnp.zeros((len(PAIRS) * xs * 2, xs * 2), F32)
    count = len(X_PARTS)
    first = [[lines[p][d] for p in range(count)] for d in range(4)]
    second = [[[line[d]] for d in range(4)] for line in lines[count:]]
    gram = add_gram(place, gram, first)
    for group in second:
        gram = add_gram(place, gram, group)
    basis = subspace(place, reduce_gram(place, gram), x_basis)

    keep0, send0 = core_of(place, basis, [first])
    came0 = pair_swap(send0, 1)
    keep1, send1 = core_of(place, basis, second)
    came1 = pair_swap(send1, 1)
    mine, theirs = (keep0, keep1), (came0, came1)
    core_tensor = jnp.stack(
        [jnp.where(core == i // 2, mine[i % 2], theirs[i % 2]) for i in range(species)]
    ).transpose(0, 3, 1, 2)
    new_basis = lax.dynamic_slice_in_dim(basis, z * xs, xs, 0)
    return new_basis, core_tensor


def orthonormal(images):
    small = jnp.dot(images.T, images, precision=HIGHEST)
    lower = jnp.linalg.cholesky(small)
    return lax.linalg.triangular_solve(lower, images, left_side=False, lower=True, transpose_a=True)


def plain_body(slab_field, x_basis, y_basis):
    y_rows = slab_field.shape[2]
    local_basis = lax.dynamic_slice_in_dim(y_basis, lax.axis_index("ba") * y_rows, y_rows, 0)
    partial_value = jnp.einsum("sxyz,yr->sxrz", slab_field, local_basis, precision=HIGHEST)
    projected = lax.psum_scatter(partial_value, "ba", scatter_dimension=3, tiled=True)
    columns = lax.all_to_all(projected, "aa", split_axis=2, concat_axis=1, tiled=True)
    basis = x_basis
    local_gram = jnp.einsum("sxrz,svrz->xv", columns, columns, precision=HIGHEST)
    gram_matrix = lax.psum(local_gram, ("aa", "ba"))
    for _ in range(ITERS):
        basis = orthonormal(jnp.dot(gram_matrix, basis, precision=HIGHEST))
    core_tensor = jnp.einsum("xk,sxrz->skrz", basis, columns, precision=HIGHEST)
    basis_rows = x_basis.shape[0] // lax.axis_size("aa")
    new_basis = lax.dynamic_slice_in_dim(basis, lax.axis_index("aa") * basis_rows, basis_rows, 0)
    return new_basis, core_tensor


def solution(mesh):
    def body(slab_field, x_basis, y_basis):
        fits = (
            mesh.shape["aa"] == 4
            and mesh.shape["ba"] == 4
            and slab_field.shape == (4, LANES, LANES, 2 * LANES)
            and x_basis.shape == y_basis.shape == (4 * LANES, LANES)
        )
        return (fast_body if fits else plain_body)(slab_field, x_basis, y_basis)

    return jax.shard_map(
        body,
        mesh=mesh,
        in_specs=(P("slab", "aa", "ba", None), P("slab", None), P("slab", None)),
        out_specs=(P(("slab", "aa"), None), P("slab", None, "aa", "ba")),
        check_vma=False,
    )
```

```python
import jax
import jax.numpy as jnp
from jax import lax
from jax.experimental import pallas as pl
from jax.experimental.pallas import tpu as pltpu
from jax.sharding import PartitionSpec as P

ITERS = 2
F32 = jnp.float32
BF16 = jnp.bfloat16
HIGHEST = lax.Precision.HIGHEST
MIB = 1 << 20
X_PARTS = (16,) * 8
R_PARTS = (4,) * 8
LANES = 128
PAIRS = ((0, 0), (1, 0), (1, 1))


def split(value):
    high = value.astype(BF16)
    return high, (value - high.astype(F32)).astype(BF16)


def nt_dot(left, right):
    return lax.dot_general(left, right, (((1,), (1,)), ((), ())), preferred_element_type=F32)


def tn_dot(left, right):
    return lax.dot_general(left, right, (((0,), (0,)), ((), ())), preferred_element_type=F32)


def in_hbm(*values):
    return [pltpu.with_memory_space_constraint(value, pltpu.HBM) for value in values]


def call(name, kernel, grid, in_specs, out_specs, out_shape, scratch=(), vmem=16):
    return pl.pallas_call(
        kernel,
        name=name,
        grid_spec=pltpu.PrefetchScalarGridSpec(
            num_scalar_prefetch=1, grid=grid, in_specs=in_specs, out_specs=out_specs, scratch_shapes=list(scratch)
        ),
        out_shape=out_shape,
        compiler_params=pltpu.CompilerParams(vmem_limit_bytes=vmem * MIB, dimension_semantics=("arbitrary",) * len(grid)),
        cost_estimate=pl.CostEstimate(flops=0, bytes_accessed=0, transcendentals=0),
    )


def project_kernel(parts, place, own_ref, other_ref, basis_ref, *rest):
    outs, basis_split = rest[:-1], rest[-1]
    keeps, sends = outs[: len(parts)], outs[len(parts) :]
    rank = basis_ref.shape[0]

    @pl.when(pl.program_id(0) == 0)
    def _():
        high, low = split(basis_ref[...])
        basis_split[0:rank, :] = high
        basis_split[rank:, :] = low

    first = place[0] == 0
    stacked = basis_split[...]
    for i in range(own_ref.shape[1]):
        high, low = split(jnp.concatenate([own_ref[0, i], other_ref[i]], axis=0))
        both = jnp.dot(stacked, high, preferred_element_type=F32)
        out = both[:rank] + (both[rank:] + jnp.dot(stacked[:rank], low, preferred_element_type=F32))
        left, right = out[:, :LANES], out[:, LANES:]
        keep, send = jnp.where(first, left, right), jnp.where(first, right, left)
        at = 0
        for a in range(4):
            for part, rows in enumerate(parts):
                keeps[part][a, :, i, :] = keep[at : at + rows]
                sends[part][a, :, i, :] = send[at : at + rows]
                at += rows


def project(place, field, other, basis, job, offset):
    species, x_start, xs, parts = job
    _, ys, zs = other.shape
    rank = basis.shape[0]
    block = 8
    steps = xs // block
    shapes = [(4, rows, xs, zs // 2) for rows in parts] * 2
    in_specs = [
        pl.BlockSpec((1, block, ys, zs), lambda i, place: (2 * place[1] + species, x_start // block + i, 0, 0)),
        pl.BlockSpec((block, ys, zs), lambda i, place: (offset // block + i, 0, 0)),
        pl.BlockSpec(basis.shape, lambda i, place: (0, 0)),
    ]
    out_specs = [pl.BlockSpec((4, s[1], block, s[3]), lambda i, place: (0, 0, i, 0)) for s in shapes]
    result = call(
        "project_k",
        lambda place, *refs: project_kernel(parts, place, *refs),
        (steps,),
        in_specs,
        out_specs,
        [pltpu.HBM(s, F32) for s in shapes],
        [pltpu.VMEM((2 * rank, 2 * ys), BF16)],
        vmem=60,
    )(place, *in_hbm(field, other), basis)
    count = len(parts)
    return result[:count], result[count:]


def add_kernel(place, keep_ref, recv_ref, *outs):
    for d in range(4):
        to = lax.bitwise_xor(place[2], d)
        outs[d][...] = keep_ref[to] + recv_ref[to]


def add_up(place, keep, recv):
    _, rows, xs, zs = keep.shape
    block = min(rows, max(1, 4 * LANES // xs))
    while rows % block:
        block -= 1
    spec = pl.BlockSpec((4, block, xs, zs), lambda i, place: (0, i, 0, 0))
    out = pl.BlockSpec((block, xs, zs), lambda i, place: (i, 0, 0))
    return call(
        "add_k",
        add_kernel,
        (rows // block,),
        [spec, spec],
        [out] * 4,
        [pltpu.HBM((rows, xs, zs), F32)] * 4,
        vmem=60,
    )(place, *in_hbm(keep, recv))


def gram_kernel(parts, place, start_ref, *rest):
    lines, (out_ref, high_ref, low_ref) = rest[: 4 * parts], rest[4 * parts :]
    rows = lines[0].shape[0]
    xs = high_ref.shape[0] // 4

    @pl.when(pl.program_id(0) == 0)
    def _():
        out_ref[...] = start_ref[...]

    for d in range(4):
        base = pl.multiple_of(lax.bitwise_xor(place[2], d) * xs, xs)
        for r in range(rows):
            block = jnp.concatenate([lines[d * parts + p][r] for p in range(parts)], axis=0)
            high, low = split(block)
            high_ref[pl.ds(base, xs), r * LANES : (r + 1) * LANES] = high
            low_ref[pl.ds(base, xs), r * LANES : (r + 1) * LANES] = low
    size = out_ref.shape[1]
    for index, (i, j) in enumerate(PAIRS):
        hi, li = high_ref[i * size : (i + 1) * size], low_ref[i * size : (i + 1) * size]
        hj, lj = high_ref[j * size : (j + 1) * size], low_ref[j * size : (j + 1) * size]
        out_ref[index * size : (index + 1) * size, :] += nt_dot(hi, hj) + (nt_dot(hi, lj) + nt_dot(li, hj))


def add_gram(place, start, lines):
    parts = len(lines[0])
    rows, _, zs = lines[0][0].shape
    block = min(8, rows)
    total = 2 * start.shape[1]
    flat = [piece for group in lines for piece in group]
    whole = pl.BlockSpec(start.shape, lambda i, place: (0, 0))
    return call(
        "gram_k",
        lambda place, *refs: gram_kernel(parts, place, *refs),
        (rows // block,),
        [whole] + [pl.BlockSpec((block, *piece.shape[1:]), lambda i, place: (i, 0, 0)) for piece in flat],
        whole,
        jax.ShapeDtypeStruct(start.shape, F32),
        [pltpu.VMEM((total, block * zs), BF16)] * 2,
        vmem=60,
    )(place, start, *in_hbm(*flat))


def inverse_factor(small):
    n = small.shape[0]
    rows = lax.broadcasted_iota(jnp.int32, (n, n), 0)
    cols = lax.broadcasted_iota(jnp.int32, (n, n), 1)
    unit = jnp.where(rows == cols, 1.0, 0.0).astype(F32)
    tiles = [small[8 * t : 8 * t + 8] for t in range(n // 8)]
    units = [unit[8 * t : 8 * t + 8] for t in range(n // 8)]
    sub = lax.broadcasted_iota(jnp.int32, (8, n), 0)
    done = [None] * (n // 8)
    for j in range(n):
        at, r = divmod(j, 8)
        row, unit_row = tiles[at][r : r + 1], units[at][r : r + 1]
        pivot = row[:, j : j + 1]
        inverse = 1.0 / pivot
        scale = lax.rsqrt(pivot)
        scaled = row * inverse
        for t in range(at, n // 8):
            column = tiles[t][:, j : j + 1]
            if t == at:
                column = jnp.where(sub[:, 0:1] > r, column, 0.0)
            factor = column * inverse
            tiles[t] = tiles[t] - factor * row
            units[t] = units[t] - factor * unit_row
        piece = jnp.where(sub == r, unit_row * scale, 0.0)
        done[at] = piece if r == 0 else done[at] + piece
    return jnp.concatenate(done, axis=0)


def basis_kernel(place, pieces_ref, start_ref, out_ref, gram_ref):
    count, size = pieces_ref.shape[0], pieces_ref.shape[1]
    for core in range(2):
        for chip in range(2):
            for d in range(4):
                at = (
                    lax.rem(place[1] + core, 2) * 8
                    + lax.rem(place[0] + chip, 2) * 4
                    + lax.bitwise_xor(place[2], d)
                )
                gram_ref[pl.ds(pl.multiple_of(at * size, 8), size), :] = pieces_ref[(core * 2 + chip) * 4 + d]
    half = gram_ref.shape[1]
    g00, g10, g11 = (gram_ref[i * half : (i + 1) * half, :] for i in range(3))
    g01 = g10.T
    basis = start_ref[...]
    for _ in range(ITERS):
        top, low = basis[:half], basis[half:]
        dot = lambda a, b: jnp.dot(a, b, precision=HIGHEST, preferred_element_type=F32)
        images = jnp.concatenate([dot(g00, top) + dot(g01, low), dot(g10, top) + dot(g11, low)], axis=0)
        small = dot(images.T, images)
        basis = dot(images, inverse_factor(small).T)
    out_ref[...] = basis


def subspace(place, pieces, start):
    count, size, width = pieces.shape
    return call(
        "subspace_k",
        basis_kernel,
        (1,),
        [
            pl.BlockSpec(pieces.shape, lambda i, place: (0, 0, 0)),
            pl.BlockSpec(start.shape, lambda i, place: (0, 0)),
        ],
        pl.BlockSpec(start.shape, lambda i, place: (0, 0)),
        jax.ShapeDtypeStruct(start.shape, F32),
        [pltpu.VMEM((count * size, width), F32)],
        vmem=60,
    )(place, pieces, start)


def core_kernel(counts, steps, place, basis_ref, *rest):
    lines, (keep_ref, send_ref, factor_ref) = rest[:-3], rest[-3:]
    rank = basis_ref.shape[1]
    xs = basis_ref.shape[0] // 4

    @pl.when(pl.program_id(0) == 0)
    def _():
        for d in range(4):
            base = pl.multiple_of(lax.bitwise_xor(place[2], d) * xs, xs)
            high, low = split(basis_ref[pl.ds(base, xs), :])
            factor_ref[d * xs : (d + 1) * xs, 0:rank] = high
            factor_ref[d * xs : (d + 1) * xs, rank:] = low

    factor = factor_ref[...]

    def work(groups):
        lines = [
            jnp.concatenate([piece[r] for piece in pieces], axis=0) for pieces in groups for r in range(pieces[0].shape[0])
        ]
        high, low = split(jnp.concatenate(lines, axis=1))
        both = tn_dot(high, factor)
        out = both[:, :rank] + (both[:, rank:] + tn_dot(low, factor[:, :rank]))
        out = out.reshape(len(lines), 2, LANES // 2, rank)
        first = place[1] == 0
        keep_ref[...] = jnp.where(first, out[:, 0], out[:, 1])
        send_ref[...] = jnp.where(first, out[:, 1], out[:, 0])

    groups, at = [], 0
    for count in counts:
        groups.append(lines[at : at + count])
        at += count
    if steps is None:
        work(groups)
    else:
        for step, members in enumerate(steps):

            @pl.when(pl.program_id(0) == step)
            def _(members=members):
                work([groups[member] for member in members])


def core_of(place, basis, lines):
    block = 8
    rank = basis.shape[1]
    groups = [[piece for d in group for piece in d] for group in lines]
    flat = [piece for group in groups for piece in group]
    rows = [group[0].shape[0] for group in groups]
    total, zs = sum(rows), flat[0].shape[2]
    if len(groups) == 1:
        steps = None
        specs = [pl.BlockSpec((block, *piece.shape[1:]), lambda i, place: (i, 0, 0)) for piece in flat]
    else:
        steps, at = [[] for _ in range(total // block)], 0
        for member, count in enumerate(rows):
            steps[at // block].append(member)
            at += count
        specs = [pl.BlockSpec(piece.shape, lambda i, place: (0, 0, 0)) for piece in flat]
    return call(
        "core_k",
        lambda place, *refs: core_kernel([len(group) for group in groups], steps, place, *refs),
        (total // block,),
        [pl.BlockSpec(basis.shape, lambda i, place: (0, 0))] + specs,
        [pl.BlockSpec((block, zs // 2, rank), lambda i, place: (i, 0, 0))] * 2,
        [pltpu.HBM((total, zs // 2, rank), F32)] * 2,
        [pltpu.VMEM((basis.shape[0], 2 * rank), BF16)],
        vmem=60,
    )(place, basis, *in_hbm(*flat))


def after(value, *earlier):
    return lax.optimization_barrier((value, *earlier))[0]


def pair_swap(value, distance):
    return lax.ppermute(value, "ba", [(i, i ^ distance) for i in range(4)])


def z_swap(value, d):
    return lax.ppermute(value, "aa", [(i, i ^ d) for i in range(4)])


def reduce_gram(place, gram):
    chip, core, z = place[0], place[1], place[2]
    rows, width = gram.shape
    halves = gram.reshape(2, rows // 2, width)
    take = lambda array, i: lax.dynamic_index_in_dim(array, i, 0, keepdims=False)
    gram = take(halves, core) + pair_swap(take(halves, 1 - core), 1)
    halves = gram.reshape(2, rows // 4, width)
    gram = take(halves, chip) + pair_swap(take(halves, 1 - chip), 2)
    blocks = gram.reshape(4, rows // 16, width)
    came = [z_swap(take(blocks, z ^ d), d) for d in (1, 2, 3)]
    gram = take(blocks, z) + came[0] + came[1] + came[2]
    gram = jnp.stack([gram] + [z_swap(gram, d) for d in (1, 2, 3)])
    gram = jnp.concatenate([gram, pair_swap(gram, 2)])
    return jnp.concatenate([gram, pair_swap(gram, 1)])


def fast_body(slab_field, x_basis, y_basis):
    rank = x_basis.shape[1]
    species, xs, ys, zs = slab_field.shape
    ba = lax.axis_index("ba")
    chip, core, z = ba // 2, ba % 2, lax.axis_index("aa")
    place = jnp.stack([chip, core, z]).astype(jnp.int32)
    rows = lambda index: lax.dynamic_slice_in_dim(y_basis, index * ys, ys, 0)
    basis_t = jnp.concatenate([rows(ba), rows(ba ^ 1)], axis=0).T

    share = rank // 4
    jobs, at = [], 0
    for size in X_PARTS:
        jobs.append((0, at, size, (share,)))
        at += size
    jobs.append((1, 0, xs, R_PARTS))
    keeps, sends, came, lines = [], [], [], []
    grams = [jnp.zeros((len(PAIRS) * xs * 2, xs * 2), F32)]
    count = len(X_PARTS)

    def spread(i):
        mine = add_up(place, keeps[i], came[i])
        line = [mine[0], None, None, None]
        for d, earlier in ((2, 1), (3, 2), (1, 3)):
            part = after(mine[d], lines[-1][earlier]) if lines else mine[d]
            line[d] = z_swap(part, d)
        lines.append(line)
        if i >= count - 1:
            group = [[old[d] for old in lines[:count]] for d in range(4)] if i == count - 1 else [[part] for part in line]
            grams.append(add_gram(place, grams[-1], group))

    def exchange(part):
        i = len(came)
        earlier = []
        if i >= 2:
            earlier = [came[i - 2]] + (lines[i - 3][1:] if i >= 3 else [])
        if i >= count + 3:
            earlier.append(grams[i - count - 2])
        came.append(pair_swap(after(part, *earlier), 2))
        if i >= 1:
            spread(i - 1)

    swaps = [(0, 0, X_PARTS[0]), (0, X_PARTS[0], xs - X_PARTS[0]), (1, 0, xs)]
    others, theirs = [], []
    for job in jobs:
        while swaps and swaps[0][:2] <= job[:2]:
            s, start, size = swaps.pop(0)
            earlier = ([], sends[:1], theirs[-1:])[len(theirs)]
            first = after(2 * (1 - core) + s, *earlier)
            theirs.append(lax.dynamic_slice(slab_field, (first, start, 0, 0), (1, size, ys, zs))[0])
            others.append((start, pair_swap(theirs[-1], 1)))
        base, other = others[-1]
        keep, send = project(place, slab_field, other, basis_t, job, job[1] - base)
        for mine, part in zip(keep, send):
            keeps.append(mine)
            sends.append(part)
            exchange(part)
    spread(len(keeps) - 1)

    first = [[line[d] for line in lines[:count]] for d in range(4)]
    second = [[[line[d]] for d in range(4)] for line in lines[count:]]
    basis = subspace(place, reduce_gram(place, grams[-1]), x_basis)

    keep0, send0 = core_of(place, basis, [first])
    came0 = pair_swap(send0, 1)
    keep1, send1 = core_of(place, basis, second)
    came1 = pair_swap(send1, 1)
    mine, theirs = (keep0, keep1), (came0, came1)
    core_tensor = jnp.stack(
        [jnp.where(core == i // 2, mine[i % 2], theirs[i % 2]) for i in range(species)]
    ).transpose(0, 3, 1, 2)
    new_basis = lax.dynamic_slice_in_dim(basis, z * xs, xs, 0)
    return new_basis, core_tensor


def orthonormal(images):
    small = jnp.dot(images.T, images, precision=HIGHEST)
    lower = jnp.linalg.cholesky(small)
    return lax.linalg.triangular_solve(lower, images, left_side=False, lower=True, transpose_a=True)


def plain_body(slab_field, x_basis, y_basis):
    y_rows = slab_field.shape[2]
    local_basis = lax.dynamic_slice_in_dim(y_basis, lax.axis_index("ba") * y_rows, y_rows, 0)
    partial_value = jnp.einsum("sxyz,yr->sxrz", slab_field, local_basis, precision=HIGHEST)
    projected = lax.psum_scatter(partial_value, "ba", scatter_dimension=3, tiled=True)
    columns = lax.all_to_all(projected, "aa", split_axis=2, concat_axis=1, tiled=True)
    basis = x_basis
    local_gram = jnp.einsum("sxrz,svrz->xv", columns, columns, precision=HIGHEST)
    gram_matrix = lax.psum(local_gram, ("aa", "ba"))
    for _ in range(ITERS):
        basis = orthonormal(jnp.dot(gram_matrix, basis, precision=HIGHEST))
    core_tensor = jnp.einsum("xk,sxrz->skrz", basis, columns, precision=HIGHEST)
    basis_rows = x_basis.shape[0] // lax.axis_size("aa")
    new_basis = lax.dynamic_slice_in_dim(basis, lax.axis_index("aa") * basis_rows, basis_rows, 0)
    return new_basis, core_tensor


def solution(mesh):
    def body(slab_field, x_basis, y_basis):
        fits = (
            mesh.shape["aa"] == 4
            and mesh.shape["ba"] == 4
            and slab_field.shape == (4, LANES, LANES, 2 * LANES)
            and x_basis.shape == y_basis.shape == (4 * LANES, LANES)
        )
        return (fast_body if fits else plain_body)(slab_field, x_basis, y_basis)

    return jax.shard_map(
        body,
        mesh=mesh,
        in_specs=(P("slab", "aa", "ba", None), P("slab", None), P("slab", None)),
        out_specs=(P(("slab", "aa"), None), P("slab", None, "aa", "ba")),
        check_vma=False,
    )
```

```python
import jax
import jax.numpy as jnp
from jax import lax
from jax.experimental import pallas as pl
from jax.experimental.pallas import tpu as pltpu
from jax.sharding import PartitionSpec as P

ITERS = 2
F32 = jnp.float32
BF16 = jnp.bfloat16
HIGHEST = lax.Precision.HIGHEST
MIB = 1 << 20
X_PARTS = (16,) * 8
R_PARTS = (4,) * 8
LANES = 128
PAIRS = ((0, 0), (1, 0), (1, 1))


def split(value):
    high = value.astype(BF16)
    return high, (value - high.astype(F32)).astype(BF16)


def nt_dot(left, right):
    return lax.dot_general(left, right, (((1,), (1,)), ((), ())), preferred_element_type=F32)


def tn_dot(left, right):
    return lax.dot_general(left, right, (((0,), (0,)), ((), ())), preferred_element_type=F32)


def in_hbm(*values):
    return [pltpu.with_memory_space_constraint(value, pltpu.HBM) for value in values]


def call(name, kernel, grid, in_specs, out_specs, out_shape, scratch=(), vmem=16):
    return pl.pallas_call(
        kernel,
        name=name,
        grid_spec=pltpu.PrefetchScalarGridSpec(
            num_scalar_prefetch=1, grid=grid, in_specs=in_specs, out_specs=out_specs, scratch_shapes=list(scratch)
        ),
        out_shape=out_shape,
        compiler_params=pltpu.CompilerParams(vmem_limit_bytes=vmem * MIB, dimension_semantics=("arbitrary",) * len(grid)),
        cost_estimate=pl.CostEstimate(flops=0, bytes_accessed=0, transcendentals=0),
    )


def project_kernel(parts, place, own_ref, other_ref, basis_ref, *rest):
    outs, basis_split = rest[:-1], rest[-1]
    keeps, sends = outs[: len(parts)], outs[len(parts) :]
    rank = basis_ref.shape[0]

    @pl.when(pl.program_id(0) == 0)
    def _():
        high, low = split(basis_ref[...])
        basis_split[0:rank, :] = high
        basis_split[rank:, :] = low

    first = place[0] == 0
    stacked = basis_split[...]
    for i in range(own_ref.shape[1]):
        high, low = split(jnp.concatenate([own_ref[0, i], other_ref[i]], axis=0))
        both = jnp.dot(stacked, high, preferred_element_type=F32)
        out = both[:rank] + (both[rank:] + jnp.dot(stacked[:rank], low, preferred_element_type=F32))
        left, right = out[:, :LANES], out[:, LANES:]
        keep, send = jnp.where(first, left, right), jnp.where(first, right, left)
        at = 0
        for a in range(4):
            for part, rows in enumerate(parts):
                keeps[part][a, :, i, :] = keep[at : at + rows]
                sends[part][a, :, i, :] = send[at : at + rows]
                at += rows


def project(place, field, other, basis, job, offset):
    species, x_start, xs, parts = job
    _, ys, zs = other.shape
    rank = basis.shape[0]
    block = 8
    steps = xs // block
    shapes = [(4, rows, xs, zs // 2) for rows in parts] * 2
    in_specs = [
        pl.BlockSpec((1, block, ys, zs), lambda i, place: (2 * place[1] + species, x_start // block + i, 0, 0)),
        pl.BlockSpec((block, ys, zs), lambda i, place: (offset // block + i, 0, 0)),
        pl.BlockSpec(basis.shape, lambda i, place: (0, 0)),
    ]
    out_specs = [pl.BlockSpec((4, s[1], block, s[3]), lambda i, place: (0, 0, i, 0)) for s in shapes]
    result = call(
        "project_k",
        lambda place, *refs: project_kernel(parts, place, *refs),
        (steps,),
        in_specs,
        out_specs,
        [jax.ShapeDtypeStruct(s, F32) for s in shapes],
        [pltpu.VMEM((2 * rank, 2 * ys), BF16)],
        vmem=18,
    )(place, field, other, basis)
    count = len(parts)
    return result[:count], result[count:]


def add_kernel(place, keep_ref, recv_ref, *outs):
    for d in range(4):
        to = lax.bitwise_xor(place[2], d)
        outs[d][...] = keep_ref[to] + recv_ref[to]


def add_up(place, keep, recv):
    _, rows, xs, zs = keep.shape
    block = min(rows, max(1, 4 * LANES // xs))
    while rows % block:
        block -= 1
    spec = pl.BlockSpec((4, block, xs, zs), lambda i, place: (0, i, 0, 0))
    out = pl.BlockSpec((block, xs, zs), lambda i, place: (i, 0, 0))
    return call(
        "add_k",
        add_kernel,
        (rows // block,),
        [spec, spec],
        [out] * 4,
        [jax.ShapeDtypeStruct((rows, xs, zs), F32)] * 4,
        vmem=12,
    )(place, keep, recv)


def gram_kernel(parts, place, start_ref, *rest):
    lines, (out_ref, high_ref, low_ref) = rest[: 4 * parts], rest[4 * parts :]
    rows = lines[0].shape[0]
    xs = high_ref.shape[0] // 4

    @pl.when(pl.program_id(0) == 0)
    def _():
        out_ref[...] = start_ref[...]

    for d in range(4):
        base = pl.multiple_of(lax.bitwise_xor(place[2], d) * xs, xs)
        for r in range(rows):
            block = jnp.concatenate([lines[d * parts + p][r] for p in range(parts)], axis=0)
            high, low = split(block)
            high_ref[pl.ds(base, xs), r * LANES : (r + 1) * LANES] = high
            low_ref[pl.ds(base, xs), r * LANES : (r + 1) * LANES] = low
    size = out_ref.shape[1]
    for index, (i, j) in enumerate(PAIRS):
        hi, li = high_ref[i * size : (i + 1) * size], low_ref[i * size : (i + 1) * size]
        hj, lj = high_ref[j * size : (j + 1) * size], low_ref[j * size : (j + 1) * size]
        out_ref[index * size : (index + 1) * size, :] += nt_dot(hi, hj) + (nt_dot(hi, lj) + nt_dot(li, hj))


def add_gram(place, start, lines):
    parts = len(lines[0])
    rows, _, zs = lines[0][0].shape
    block = min(8, rows)
    total = 2 * start.shape[1]
    flat = [piece for group in lines for piece in group]
    whole = pl.BlockSpec(start.shape, lambda i, place: (0, 0))
    return call(
        "gram_k",
        lambda place, *refs: gram_kernel(parts, place, *refs),
        (rows // block,),
        [whole] + [pl.BlockSpec((block, *piece.shape[1:]), lambda i, place: (i, 0, 0)) for piece in flat],
        whole,
        jax.ShapeDtypeStruct(start.shape, F32),
        [pltpu.VMEM((total, block * zs), BF16)] * 2,
        vmem=20,
    )(place, start, *in_hbm(*flat))


def inverse_factor(small):
    n = small.shape[0]
    shape = (8, n)
    rows = lax.broadcasted_iota(jnp.int32, (n, n), 0)
    cols = lax.broadcasted_iota(jnp.int32, (n, n), 1)
    unit = jnp.where(rows == cols, 1.0, 0.0).astype(F32)
    tiles = [small[t : t + 8] for t in range(0, n, 8)]
    units = [unit[t : t + 8] for t in range(0, n, 8)]
    sub = lax.broadcasted_iota(jnp.int32, shape, 0)
    along_row = lambda tile, j: jnp.broadcast_to(tile[:, j : j + 1], shape)
    spread = lambda tile, i: jnp.broadcast_to(tile[i : i + 1], shape)
    done = []
    for b in range(n // 8):
        columns = [along_row(tiles[b], 8 * b + k) for k in range(8)]
        entry = [[spread(columns[k], i) if i >= k else None for k in range(8)] for i in range(8)]
        row = [spread(tiles[b], i) for i in range(8)]
        unit_row = [spread(units[b], i) for i in range(8)]
        inverse, factor = [None] * 8, [[None] * 8 for _ in range(8)]
        for k in range(8):
            inverse[k] = 1.0 / entry[k][k]
            for i in range(k + 1, 8):
                factor[i][k] = entry[i][k] * inverse[k]
                for j in range(k + 1, i + 1):
                    entry[i][j] = entry[i][j] - factor[i][k] * entry[j][k]
                row[i] = row[i] - factor[i][k] * row[k]
                unit_row[i] = unit_row[i] - factor[i][k] * unit_row[k]
        result = jnp.zeros(shape, F32)
        for k in range(8):
            result = jnp.where(sub == k, unit_row[k] * lax.rsqrt(entry[k][k]), result)
        done.append(result)
        for t in range(b + 1, n // 8):
            column = [along_row(tiles[t], 8 * b + k) for k in range(8)]
            for k in range(8):
                for m in range(k):
                    column[k] = column[k] - factor[k][m] * column[m]
                scaled = column[k] * inverse[k]
                tiles[t] = tiles[t] - scaled * row[k]
                units[t] = units[t] - scaled * unit_row[k]
    return jnp.concatenate(done, axis=0)


def basis_kernel(place, pieces_ref, start_ref, out_ref, gram_ref):
    count, size = pieces_ref.shape[0], pieces_ref.shape[1]
    for core in range(2):
        for chip in range(2):
            for d in range(4):
                at = (
                    lax.rem(place[1] + core, 2) * 8
                    + lax.rem(place[0] + chip, 2) * 4
                    + lax.bitwise_xor(place[2], d)
                )
                gram_ref[pl.ds(pl.multiple_of(at * size, 8), size), :] = pieces_ref[(core * 2 + chip) * 4 + d]
    half = gram_ref.shape[1]
    g00, g10, g11 = (gram_ref[i * half : (i + 1) * half, :] for i in range(3))
    g01 = g10.T
    dot = lambda a, b: jnp.dot(a, b, precision=HIGHEST, preferred_element_type=F32)
    out_ref[...] = start_ref[...]

    def iterate(_, carry):
        top, low = out_ref[:half], out_ref[half:]
        images = jnp.concatenate([dot(g00, top) + dot(g01, low), dot(g10, top) + dot(g11, low)], axis=0)
        small = dot(images.T, images)
        out_ref[...] = dot(images, inverse_factor(small).T)
        return carry

    lax.fori_loop(0, ITERS, iterate, 0)


def subspace(place, pieces, start):
    count, size, width = pieces.shape
    return call(
        "subspace_k",
        basis_kernel,
        (1,),
        [
            pl.BlockSpec(pieces.shape, lambda i, place: (0, 0, 0)),
            pl.BlockSpec(start.shape, lambda i, place: (0, 0)),
        ],
        pl.BlockSpec(start.shape, lambda i, place: (0, 0)),
        jax.ShapeDtypeStruct(start.shape, F32),
        [pltpu.VMEM((count * size, width), F32)],
        vmem=12,
    )(place, pieces, start)


def core_kernel(counts, steps, place, basis_ref, *rest):
    lines, (keep_ref, send_ref, factor_ref) = rest[:-3], rest[-3:]
    rank = basis_ref.shape[1]
    xs = basis_ref.shape[0] // 4

    @pl.when(pl.program_id(0) == 0)
    def _():
        for d in range(4):
            base = pl.multiple_of(lax.bitwise_xor(place[2], d) * xs, xs)
            high, low = split(basis_ref[pl.ds(base, xs), :])
            factor_ref[d * xs : (d + 1) * xs, 0:rank] = high
            factor_ref[d * xs : (d + 1) * xs, rank:] = low

    factor = factor_ref[...]

    def work(groups):
        lines = [
            jnp.concatenate([piece[r] for piece in pieces], axis=0) for pieces in groups for r in range(pieces[0].shape[0])
        ]
        high, low = split(jnp.concatenate(lines, axis=1))
        both = tn_dot(high, factor)
        out = both[:, :rank] + (both[:, rank:] + tn_dot(low, factor[:, :rank]))
        out = out.reshape(len(lines), 2, LANES // 2, rank)
        first = place[1] == 0
        keep_ref[...] = jnp.where(first, out[:, 0], out[:, 1])
        send_ref[...] = jnp.where(first, out[:, 1], out[:, 0])

    groups, at = [], 0
    for count in counts:
        groups.append(lines[at : at + count])
        at += count
    if steps is None:
        work(groups)
    else:
        for step, members in enumerate(steps):

            @pl.when(pl.program_id(0) == step)
            def _(members=members):
                work([groups[member] for member in members])


def core_of(place, basis, lines):
    block = 8
    rank = basis.shape[1]
    groups = [[piece for d in group for piece in d] for group in lines]
    flat = [piece for group in groups for piece in group]
    rows = [group[0].shape[0] for group in groups]
    total, zs = sum(rows), flat[0].shape[2]
    if len(groups) == 1:
        steps = None
        specs = [pl.BlockSpec((block, *piece.shape[1:]), lambda i, place: (i, 0, 0)) for piece in flat]
    else:
        steps, at = [[] for _ in range(total // block)], 0
        for member, count in enumerate(rows):
            steps[at // block].append(member)
            at += count
        specs = [pl.BlockSpec(piece.shape, lambda i, place: (0, 0, 0)) for piece in flat]
    return call(
        "core_k",
        lambda place, *refs: core_kernel([len(group) for group in groups], steps, place, *refs),
        (total // block,),
        [pl.BlockSpec(basis.shape, lambda i, place: (0, 0))] + specs,
        [pl.BlockSpec((block, zs // 2, rank), lambda i, place: (i, 0, 0))] * 2,
        [pltpu.HBM((total, zs // 2, rank), F32)] * 2,
        [pltpu.VMEM((basis.shape[0], 2 * rank), BF16)],
        vmem=36,
    )(place, basis, *in_hbm(*flat))


def after(value, *earlier):
    return lax.optimization_barrier((value, *earlier))[0]


def pair_swap(value, distance):
    return lax.ppermute(value, "ba", [(i, i ^ distance) for i in range(4)])


def z_swap(value, d):
    return lax.ppermute(value, "aa", [(i, i ^ d) for i in range(4)])


def reduce_gram(place, gram):
    chip, core, z = place[0], place[1], place[2]
    rows, width = gram.shape
    halves = gram.reshape(2, rows // 2, width)
    take = lambda array, i: lax.dynamic_index_in_dim(array, i, 0, keepdims=False)
    gram = take(halves, core) + pair_swap(take(halves, 1 - core), 1)
    halves = gram.reshape(2, rows // 4, width)
    gram = take(halves, chip) + pair_swap(take(halves, 1 - chip), 2)
    blocks = gram.reshape(4, rows // 16, width)
    came = [z_swap(take(blocks, z ^ d), d) for d in (1, 2, 3)]
    gram = take(blocks, z) + came[0] + came[1] + came[2]
    gram = jnp.stack([gram] + [z_swap(gram, d) for d in (1, 2, 3)])
    gram = jnp.concatenate([gram, pair_swap(gram, 2)])
    return jnp.concatenate([gram, pair_swap(gram, 1)])


def fast_body(slab_field, x_basis, y_basis):
    rank = x_basis.shape[1]
    species, xs, ys, zs = slab_field.shape
    ba = lax.axis_index("ba")
    chip, core, z = ba // 2, ba % 2, lax.axis_index("aa")
    place = jnp.stack([chip, core, z]).astype(jnp.int32)
    rows = lambda index: lax.dynamic_slice_in_dim(y_basis, index * ys, ys, 0)
    basis_t = jnp.concatenate([rows(ba), rows(ba ^ 1)], axis=0).T

    share = rank // 4
    jobs, at = [], 0
    for size in X_PARTS:
        jobs.append((0, at, size, (share,)))
        at += size
    jobs.append((1, 0, xs, R_PARTS))
    keeps, sends, came, lines = [], [], [], []
    grams = [jnp.zeros((len(PAIRS) * xs * 2, xs * 2), F32)]
    count = len(X_PARTS)

    def spread(i):
        mine = add_up(place, keeps[i], came[i])
        line = [mine[0], None, None, None]
        for d, earlier in ((2, 1), (3, 2), (1, 3)):
            part = after(mine[d], lines[-1][earlier]) if lines else mine[d]
            line[d] = z_swap(part, d)
        lines.append(line)
        if i >= count - 1:
            group = [[old[d] for old in lines[:count]] for d in range(4)] if i == count - 1 else [[part] for part in line]
            grams.append(add_gram(place, grams[-1], group))

    def exchange(part):
        i = len(came)
        earlier = []
        if i >= 2:
            earlier = [came[i - 2]] + (lines[i - 3][1:] if i >= 3 else [])
        if i >= count + 3:
            earlier.append(grams[i - count - 2])
        came.append(pair_swap(after(part, *earlier), 2))
        if i >= 1:
            spread(i - 1)

    swaps = [(0, 0, X_PARTS[0]), (0, X_PARTS[0], xs - X_PARTS[0]), (1, 0, xs)]
    others, theirs = [], []
    for job in jobs:
        while swaps and swaps[0][:2] <= job[:2]:
            s, start, size = swaps.pop(0)
            earlier = ([], sends[:1], theirs[-1:])[len(theirs)]
            first = after(2 * (1 - core) + s, *earlier)
            theirs.append(lax.dynamic_slice(slab_field, (first, start, 0, 0), (1, size, ys, zs))[0])
            others.append((start, pair_swap(theirs[-1], 1)))
        base, other = others[-1]
        keep, send = project(place, slab_field, other, basis_t, job, job[1] - base)
        for mine, part in zip(keep, send):
            keeps.append(mine)
            sends.append(part)
            exchange(part)
    spread(len(keeps) - 1)

    first = [[line[d] for line in lines[:count]] for d in range(4)]
    second = [[[line[d]] for d in range(4)] for line in lines[count:]]
    basis = subspace(place, reduce_gram(place, grams[-1]), x_basis)

    keep0, send0 = core_of(place, basis, [first])
    came0 = pair_swap(send0, 1)
    keep1, send1 = core_of(place, basis, second)
    came1 = pair_swap(send1, 1)
    mine, theirs = (keep0, keep1), (came0, came1)
    core_tensor = jnp.stack(
        [jnp.where(core == i // 2, mine[i % 2], theirs[i % 2]) for i in range(species)]
    ).transpose(0, 3, 1, 2)
    new_basis = lax.dynamic_slice_in_dim(basis, z * xs, xs, 0)
    return new_basis, core_tensor


def orthonormal(images):
    small = jnp.dot(images.T, images, precision=HIGHEST)
    lower = jnp.linalg.cholesky(small)
    return lax.linalg.triangular_solve(lower, images, left_side=False, lower=True, transpose_a=True)


def plain_body(slab_field, x_basis, y_basis):
    y_rows = slab_field.shape[2]
    local_basis = lax.dynamic_slice_in_dim(y_basis, lax.axis_index("ba") * y_rows, y_rows, 0)
    partial_value = jnp.einsum("sxyz,yr->sxrz", slab_field, local_basis, precision=HIGHEST)
    projected = lax.psum_scatter(partial_value, "ba", scatter_dimension=3, tiled=True)
    columns = lax.all_to_all(projected, "aa", split_axis=2, concat_axis=1, tiled=True)
    basis = x_basis
    local_gram = jnp.einsum("sxrz,svrz->xv", columns, columns, precision=HIGHEST)
    gram_matrix = lax.psum(local_gram, ("aa", "ba"))
    for _ in range(ITERS):
        basis = orthonormal(jnp.dot(gram_matrix, basis, precision=HIGHEST))
    core_tensor = jnp.einsum("xk,sxrz->skrz", basis, columns, precision=HIGHEST)
    basis_rows = x_basis.shape[0] // lax.axis_size("aa")
    new_basis = lax.dynamic_slice_in_dim(basis, lax.axis_index("aa") * basis_rows, basis_rows, 0)
    return new_basis, core_tensor


def solution(mesh):
    def body(slab_field, x_basis, y_basis):
        fits = (
            mesh.shape["aa"] == 4
            and mesh.shape["ba"] == 4
            and slab_field.shape == (4, LANES, LANES, 2 * LANES)
            and x_basis.shape == y_basis.shape == (4 * LANES, LANES)
        )
        return (fast_body if fits else plain_body)(slab_field, x_basis, y_basis)

    return jax.shard_map(
        body,
        mesh=mesh,
        in_specs=(P("slab", "aa", "ba", None), P("slab", None), P("slab", None)),
        out_specs=(P(("slab", "aa"), None), P("slab", None, "aa", "ba")),
        check_vma=False,
    )
```

```python
import jax
import jax.numpy as jnp
from jax import lax
from jax.experimental import pallas as pl
from jax.experimental.pallas import tpu as pltpu
from jax.sharding import PartitionSpec as P

ITERS = 2
F32 = jnp.float32
BF16 = jnp.bfloat16
HIGHEST = lax.Precision.HIGHEST
MIB = 1 << 20
X_PARTS = (16,) * 8
R_PARTS = (4,) * 8
LANES = 128
PAIRS = ((0, 0), (1, 0), (1, 1))


def split(value):
    high = value.astype(BF16)
    return high, (value - high.astype(F32)).astype(BF16)


def nt_dot(left, right):
    return lax.dot_general(left, right, (((1,), (1,)), ((), ())), preferred_element_type=F32)


def tn_dot(left, right):
    return lax.dot_general(left, right, (((0,), (0,)), ((), ())), preferred_element_type=F32)


def in_hbm(*values):
    return [pltpu.with_memory_space_constraint(value, pltpu.HBM) for value in values]


def call(name, kernel, grid, in_specs, out_specs, out_shape, scratch=(), vmem=16, aliases={}):
    return pl.pallas_call(
        kernel,
        name=name,
        grid_spec=pltpu.PrefetchScalarGridSpec(
            num_scalar_prefetch=1, grid=grid, in_specs=in_specs, out_specs=out_specs, scratch_shapes=list(scratch)
        ),
        out_shape=out_shape,
        input_output_aliases=aliases,
        compiler_params=pltpu.CompilerParams(vmem_limit_bytes=vmem * MIB, dimension_semantics=("arbitrary",) * len(grid)),
        cost_estimate=pl.CostEstimate(flops=0, bytes_accessed=0, transcendentals=0),
    )


def project_kernel(parts, skip, place, own_ref, other_ref, basis_ref, *rest):
    outs, basis_split = rest[skip:-1], rest[-1]
    keeps, sends = outs[: len(parts)], outs[len(parts) :]
    rank = basis_ref.shape[0]

    @pl.when(pl.program_id(0) == 0)
    def _():
        high, low = split(basis_ref[...])
        basis_split[0:rank, :] = high
        basis_split[rank:, :] = low

    first = place[0] == 0
    stacked = basis_split[...]
    for i in range(own_ref.shape[1]):
        high, low = split(jnp.concatenate([own_ref[0, i], other_ref[i]], axis=0))
        both = jnp.dot(stacked, high, preferred_element_type=F32)
        out = both[:rank] + (both[rank:] + jnp.dot(stacked[:rank], low, preferred_element_type=F32))
        left, right = out[:, :LANES], out[:, LANES:]
        keep, send = jnp.where(first, left, right), jnp.where(first, right, left)
        at = 0
        for a in range(4):
            for part, rows in enumerate(parts):
                keeps[part][a, :, i, :] = keep[at : at + rows]
                sends[part][a, :, i, :] = send[at : at + rows]
                at += rows


def project(place, field, other, basis, job, offset, total, before):
    species, x_start, xs, parts = job
    _, ys, zs = other.shape
    rank = basis.shape[0]
    block = 8
    steps = xs // block
    shapes = [(4, rows, total, zs // 2) for rows in parts] * 2
    first = x_start // block if total > xs else 0
    array = pltpu.HBM if total > xs else jax.ShapeDtypeStruct
    in_specs = [
        pl.BlockSpec((1, block, ys, zs), lambda i, place: (2 * place[1] + species, x_start // block + i, 0, 0)),
        pl.BlockSpec((block, ys, zs), lambda i, place: (offset // block + i, 0, 0)),
        pl.BlockSpec(basis.shape, lambda i, place: (0, 0)),
    ] + [pl.BlockSpec(memory_space=pl.ANY)] * len(before)
    out_specs = [pl.BlockSpec((4, s[1], block, s[3]), lambda i, place: (0, 0, first + i, 0)) for s in shapes]
    result = call(
        "project_k",
        lambda place, *refs: project_kernel(parts, len(before), place, *refs),
        (steps,),
        in_specs,
        out_specs,
        [array(s, F32) for s in shapes],
        [pltpu.VMEM((2 * rank, 2 * ys), BF16)],
        vmem=18,
        aliases={4 + index: index for index in range(len(before))},
    )(place, field, other, basis, *in_hbm(*before))
    count = len(parts)
    return result[:count], result[count:]


def add_kernel(place, keep_ref, recv_ref, *outs):
    for d in range(4):
        to = lax.bitwise_xor(place[2], d)
        outs[d][...] = keep_ref[to] + recv_ref[to]


def add_up(place, keep, recv):
    _, rows, xs, zs = keep.shape
    block = min(rows, max(1, 4 * LANES // xs))
    while rows % block:
        block -= 1
    spec = pl.BlockSpec((4, block, xs, zs), lambda i, place: (0, i, 0, 0))
    out = pl.BlockSpec((block, xs, zs), lambda i, place: (i, 0, 0))
    return call(
        "add_k",
        add_kernel,
        (rows // block,),
        [spec, spec],
        [out] * 4,
        [jax.ShapeDtypeStruct((rows, xs, zs), F32)] * 4,
        vmem=12,
    )(place, keep, recv)


def gram_kernel(parts, place, start_ref, *rest):
    lines, (out_ref, high_ref, low_ref) = rest[: 4 * parts], rest[4 * parts :]
    rows = lines[0].shape[0]
    xs = high_ref.shape[0] // 4

    @pl.when(pl.program_id(0) == 0)
    def _():
        out_ref[...] = start_ref[...]

    for d in range(4):
        base = pl.multiple_of(lax.bitwise_xor(place[2], d) * xs, xs)
        for r in range(rows):
            block = jnp.concatenate([lines[d * parts + p][r] for p in range(parts)], axis=0)
            high, low = split(block)
            high_ref[pl.ds(base, xs), r * LANES : (r + 1) * LANES] = high
            low_ref[pl.ds(base, xs), r * LANES : (r + 1) * LANES] = low
    size = out_ref.shape[1]
    for index, (i, j) in enumerate(PAIRS):
        hi, li = high_ref[i * size : (i + 1) * size], low_ref[i * size : (i + 1) * size]
        hj, lj = high_ref[j * size : (j + 1) * size], low_ref[j * size : (j + 1) * size]
        out_ref[index * size : (index + 1) * size, :] += nt_dot(hi, hj) + (nt_dot(hi, lj) + nt_dot(li, hj))


def add_gram(place, start, lines):
    parts = len(lines[0])
    rows, _, zs = lines[0][0].shape
    block = min(8, rows)
    total = 2 * start.shape[1]
    flat = [piece for group in lines for piece in group]
    whole = pl.BlockSpec(start.shape, lambda i, place: (0, 0))
    return call(
        "gram_k",
        lambda place, *refs: gram_kernel(parts, place, *refs),
        (rows // block,),
        [whole] + [pl.BlockSpec((block, *piece.shape[1:]), lambda i, place: (i, 0, 0)) for piece in flat],
        whole,
        jax.ShapeDtypeStruct(start.shape, F32),
        [pltpu.VMEM((total, block * zs), BF16)] * 2,
        vmem=20,
    )(place, start, *in_hbm(*flat))


def inverse_factor(small):
    n = small.shape[0]
    shape = (8, n)
    rows = lax.broadcasted_iota(jnp.int32, (n, n), 0)
    cols = lax.broadcasted_iota(jnp.int32, (n, n), 1)
    unit = jnp.where(rows == cols, 1.0, 0.0).astype(F32)
    tiles = [small[t : t + 8] for t in range(0, n, 8)]
    units = [unit[t : t + 8] for t in range(0, n, 8)]
    sub = lax.broadcasted_iota(jnp.int32, shape, 0)
    along_row = lambda tile, j: jnp.broadcast_to(tile[:, j : j + 1], shape)
    spread = lambda tile, i: jnp.broadcast_to(tile[i : i + 1], shape)
    done = []
    for b in range(n // 8):
        columns = [along_row(tiles[b], 8 * b + k) for k in range(8)]
        entry = [[spread(columns[k], i) if i >= k else None for k in range(8)] for i in range(8)]
        row = [spread(tiles[b], i) for i in range(8)]
        unit_row = [spread(units[b], i) for i in range(8)]
        inverse, factor = [None] * 8, [[None] * 8 for _ in range(8)]
        for k in range(8):
            inverse[k] = 1.0 / entry[k][k]
            for i in range(k + 1, 8):
                factor[i][k] = entry[i][k] * inverse[k]
                for j in range(k + 1, i + 1):
                    entry[i][j] = entry[i][j] - factor[i][k] * entry[j][k]
                row[i] = row[i] - factor[i][k] * row[k]
                unit_row[i] = unit_row[i] - factor[i][k] * unit_row[k]
        result = jnp.zeros(shape, F32)
        for k in range(8):
            result = jnp.where(sub == k, unit_row[k] * lax.rsqrt(entry[k][k]), result)
        done.append(result)
        for t in range(b + 1, n // 8):
            column = [along_row(tiles[t], 8 * b + k) for k in range(8)]
            for k in range(8):
                for m in range(k):
                    column[k] = column[k] - factor[k][m] * column[m]
                scaled = column[k] * inverse[k]
                tiles[t] = tiles[t] - scaled * row[k]
                units[t] = units[t] - scaled * unit_row[k]
    return jnp.concatenate(done, axis=0)


def basis_kernel(place, pieces_ref, start_ref, out_ref, gram_ref):
    count, size = pieces_ref.shape[0], pieces_ref.shape[1]
    for core in range(2):
        for chip in range(2):
            for d in range(4):
                at = (
                    lax.rem(place[1] + core, 2) * 8
                    + lax.rem(place[0] + chip, 2) * 4
                    + lax.bitwise_xor(place[2], d)
                )
                gram_ref[pl.ds(pl.multiple_of(at * size, 8), size), :] = pieces_ref[(core * 2 + chip) * 4 + d]
    half = gram_ref.shape[1]
    g00, g10, g11 = (gram_ref[i * half : (i + 1) * half, :] for i in range(3))
    g01 = g10.T
    dot = lambda a, b: jnp.dot(a, b, precision=HIGHEST, preferred_element_type=F32)
    out_ref[...] = start_ref[...]

    def iterate(_, carry):
        top, low = out_ref[:half], out_ref[half:]
        images = jnp.concatenate([dot(g00, top) + dot(g01, low), dot(g10, top) + dot(g11, low)], axis=0)
        small = dot(images.T, images)
        out_ref[...] = dot(images, inverse_factor(small).T)
        return carry

    lax.fori_loop(0, ITERS, iterate, 0)


def subspace(place, pieces, start):
    count, size, width = pieces.shape
    return call(
        "subspace_k",
        basis_kernel,
        (1,),
        [
            pl.BlockSpec(pieces.shape, lambda i, place: (0, 0, 0)),
            pl.BlockSpec(start.shape, lambda i, place: (0, 0)),
        ],
        pl.BlockSpec(start.shape, lambda i, place: (0, 0)),
        jax.ShapeDtypeStruct(start.shape, F32),
        [pltpu.VMEM((count * size, width), F32)],
        vmem=12,
    )(place, pieces, start)


def core_kernel(counts, steps, place, basis_ref, *rest):
    lines, (keep_ref, send_ref, factor_ref) = rest[: sum(counts)], rest[-3:]
    rank = basis_ref.shape[1]
    xs = basis_ref.shape[0] // 4

    @pl.when(pl.program_id(0) == 0)
    def _():
        for d in range(4):
            base = pl.multiple_of(lax.bitwise_xor(place[2], d) * xs, xs)
            high, low = split(basis_ref[pl.ds(base, xs), :])
            factor_ref[d * xs : (d + 1) * xs, 0:rank] = high
            factor_ref[d * xs : (d + 1) * xs, rank:] = low

    factor = factor_ref[...]

    def work(groups):
        lines = [
            jnp.concatenate([piece[r] for piece in pieces], axis=0) for pieces in groups for r in range(pieces[0].shape[0])
        ]
        high, low = split(jnp.concatenate(lines, axis=1))
        both = tn_dot(high, factor)
        out = both[:, :rank] + (both[:, rank:] + tn_dot(low, factor[:, :rank]))
        out = out.reshape(len(lines), 2, LANES // 2, rank)
        first = place[1] == 0
        keep_ref[0] = jnp.where(first, out[:, 0], out[:, 1])
        send_ref[...] = jnp.where(first, out[:, 1], out[:, 0])

    groups, at = [], 0
    for count in counts:
        groups.append(lines[at : at + count])
        at += count
    if steps is None:
        work(groups)
    else:
        for step, members in enumerate(steps):

            @pl.when(pl.program_id(0) == step)
            def _(members=members):
                work([groups[member] for member in members])


def core_of(place, basis, lines, species, whole):
    block = 8
    rank = basis.shape[1]
    groups = [[piece for d in group for piece in d] for group in lines]
    flat = [piece for group in groups for piece in group]
    rows = [group[0].shape[0] for group in groups]
    total, zs = sum(rows), flat[0].shape[2]
    before = [] if whole is None else [whole]
    if len(groups) == 1:
        steps = None
        specs = [pl.BlockSpec((block, *piece.shape[1:]), lambda i, place: (i, 0, 0)) for piece in flat]
    else:
        steps, at = [[] for _ in range(total // block)], 0
        for member, count in enumerate(rows):
            steps[at // block].append(member)
            at += count
        specs = [pl.BlockSpec(piece.shape, lambda i, place: (0, 0, 0)) for piece in flat]
    return call(
        "core_k",
        lambda place, *refs: core_kernel([len(group) for group in groups], steps, place, *refs),
        (total // block,),
        [pl.BlockSpec(basis.shape, lambda i, place: (0, 0))] + specs + [pl.BlockSpec(memory_space=pl.ANY)] * len(before),
        [
            pl.BlockSpec((1, block, zs // 2, rank), lambda i, place: (2 * place[1] + species, i, 0, 0)),
            pl.BlockSpec((block, zs // 2, rank), lambda i, place: (i, 0, 0)),
        ],
        [pltpu.HBM((4, total, zs // 2, rank), F32), pltpu.HBM((total, zs // 2, rank), F32)],
        [pltpu.VMEM((basis.shape[0], 2 * rank), BF16)],
        vmem=36,
        aliases={2 + len(flat): 0} if before else {},
    )(place, basis, *in_hbm(*flat, *before))


def finish_kernel(place, whole_ref, *refs):
    out_ref = refs[-1]
    for species, ref in enumerate(refs[:-1]):
        out_ref[species] = ref[...]


def finish(place, whole, came):
    rows, zs, rank = came[0].shape
    block = 8
    return call(
        "finish_k",
        finish_kernel,
        (rows // block,),
        [pl.BlockSpec(memory_space=pl.ANY)] + [pl.BlockSpec((block, zs, rank), lambda i, place: (i, 0, 0))] * 2,
        pl.BlockSpec((2, block, zs, rank), lambda i, place: (1 - place[1], i, 0, 0)),
        pltpu.HBM(whole.shape, F32),
        aliases={1: 0},
    )(place, *in_hbm(whole, *came))


def after(value, *earlier):
    return lax.optimization_barrier((value, *earlier))[0]


def pair_swap(value, distance):
    return lax.ppermute(value, "ba", [(i, i ^ distance) for i in range(4)])


def z_swap(value, d):
    return lax.ppermute(value, "aa", [(i, i ^ d) for i in range(4)])


def reduce_gram(place, gram):
    chip, core, z = place[0], place[1], place[2]
    rows, width = gram.shape
    halves = gram.reshape(2, rows // 2, width)
    take = lambda array, i: lax.dynamic_index_in_dim(array, i, 0, keepdims=False)
    gram = take(halves, core) + pair_swap(take(halves, 1 - core), 1)
    halves = gram.reshape(2, rows // 4, width)
    gram = take(halves, chip) + pair_swap(take(halves, 1 - chip), 2)
    blocks = gram.reshape(4, rows // 16, width)
    came = [z_swap(take(blocks, z ^ d), d) for d in (1, 2, 3)]
    gram = take(blocks, z) + came[0] + came[1] + came[2]
    gram = jnp.stack([gram] + [z_swap(gram, d) for d in (1, 2, 3)])
    gram = jnp.concatenate([gram, pair_swap(gram, 2)])
    return jnp.concatenate([gram, pair_swap(gram, 1)])


def fast_body(slab_field, x_basis, y_basis):
    rank = x_basis.shape[1]
    species, xs, ys, zs = slab_field.shape
    ba = lax.axis_index("ba")
    chip, core, z = ba // 2, ba % 2, lax.axis_index("aa")
    place = jnp.stack([chip, core, z]).astype(jnp.int32)
    rows = lambda index: lax.dynamic_slice_in_dim(y_basis, index * ys, ys, 0)
    basis_t = jnp.concatenate([rows(ba), rows(ba ^ 1)], axis=0).T

    share = rank // 4
    jobs, at = [], 0
    for size in X_PARTS:
        jobs.append((0, at, size, (share,)))
        at += size
    late = [(1, start, xs // 2, R_PARTS) for start in (0, xs // 2)]
    jobs[3:3] = late
    keeps, sends, came, lines = [], [], [], []
    halves = []
    grams = [jnp.zeros((len(PAIRS) * xs * 2, xs * 2), F32)]
    count = len(X_PARTS)

    def spread(i):
        mine = add_up(place, keeps[i], came[i])
        line = [mine[0], None, None, None]
        for d, earlier in ((2, 1), (3, 2), (1, 3)):
            part = after(mine[d], lines[-1][earlier]) if lines else mine[d]
            line[d] = z_swap(part, d)
        lines.append(line)
        if i >= count - 1:
            group = [[old[d] for old in lines[:count]] for d in range(4)] if i == count - 1 else [[part] for part in line]
            grams.append(add_gram(place, grams[-1], group))

    def exchange(part):
        i = len(came)
        earlier = []
        if i >= 2:
            earlier = [came[i - 2]] + (lines[i - 3][1:] if i >= 3 else [])
        if i in (6, 7):
            earlier.append(halves[i - 6])
        if i >= count + 3:
            earlier.append(grams[i - count - 2])
        came.append(pair_swap(after(part, *earlier), 2))
        if i >= 1:
            spread(i - 1)

    swaps = [(0, 0, X_PARTS[0]), (0, X_PARTS[0], xs - X_PARTS[0]), (1, 0, xs)]
    others, theirs, second = [], [], []
    for job in jobs:
        while swaps and swaps[0][0] <= job[0] and swaps[0][1] <= job[1]:
            s, start, size = swaps.pop(0)
            earlier = ([], sends[:1], lines[0][:1] if lines else [])[len(theirs)]
            first = after(2 * (1 - core) + s, *earlier)
            theirs.append(lax.dynamic_slice(slab_field, (first, start, 0, 0), (1, size, ys, zs))[0])
            others.append((s, start, pair_swap(theirs[-1], 1)))
        base, other = [(start, array) for s, start, array in others if s == job[0] and start <= job[1]][-1]
        if job[0] == 0:
            keep, send = project(place, slab_field, other, basis_t, job, job[1] - base, job[2], [])
        else:
            keep, send = project(place, slab_field, other, basis_t, job, job[1] - base, xs, second)
            second = [*keep, *send]
            halves.append(send[0])
            continue
        for mine, part in zip(keep, send):
            keeps.append(mine)
            sends.append(part)
            exchange(part)
    for mine, part in zip(second[: len(R_PARTS)], second[len(R_PARTS) :]):
        keeps.append(mine)
        sends.append(part)
        exchange(part)
    spread(len(keeps) - 1)

    first = [[line[d] for line in lines[:count]] for d in range(4)]
    second = [[[line[d]] for d in range(4)] for line in lines[count:]]
    basis = subspace(place, reduce_gram(place, grams[-1]), x_basis)

    whole, send0 = core_of(place, basis, [first], 0, None)
    came0 = pair_swap(send0, 1)
    whole, send1 = core_of(place, basis, second, 1, whole)
    core_tensor = finish(place, whole, [came0, pair_swap(send1, 1)]).transpose(0, 3, 1, 2)
    new_basis = lax.dynamic_slice_in_dim(basis, z * xs, xs, 0)
    return new_basis, core_tensor


def orthonormal(images):
    small = jnp.dot(images.T, images, precision=HIGHEST)
    lower = jnp.linalg.cholesky(small)
    return lax.linalg.triangular_solve(lower, images, left_side=False, lower=True, transpose_a=True)


def plain_body(slab_field, x_basis, y_basis):
    y_rows = slab_field.shape[2]
    local_basis = lax.dynamic_slice_in_dim(y_basis, lax.axis_index("ba") * y_rows, y_rows, 0)
    partial_value = jnp.einsum("sxyz,yr->sxrz", slab_field, local_basis, precision=HIGHEST)
    projected = lax.psum_scatter(partial_value, "ba", scatter_dimension=3, tiled=True)
    columns = lax.all_to_all(projected, "aa", split_axis=2, concat_axis=1, tiled=True)
    basis = x_basis
    local_gram = jnp.einsum("sxrz,svrz->xv", columns, columns, precision=HIGHEST)
    gram_matrix = lax.psum(local_gram, ("aa", "ba"))
    for _ in range(ITERS):
        basis = orthonormal(jnp.dot(gram_matrix, basis, precision=HIGHEST))
    core_tensor = jnp.einsum("xk,sxrz->skrz", basis, columns, precision=HIGHEST)
    basis_rows = x_basis.shape[0] // lax.axis_size("aa")
    new_basis = lax.dynamic_slice_in_dim(basis, lax.axis_index("aa") * basis_rows, basis_rows, 0)
    return new_basis, core_tensor


def solution(mesh):
    def body(slab_field, x_basis, y_basis):
        fits = (
            mesh.shape["aa"] == 4
            and mesh.shape["ba"] == 4
            and slab_field.shape == (4, LANES, LANES, 2 * LANES)
            and x_basis.shape == y_basis.shape == (4 * LANES, LANES)
        )
        return (fast_body if fits else plain_body)(slab_field, x_basis, y_basis)

    return jax.shard_map(
        body,
        mesh=mesh,
        in_specs=(P("slab", "aa", "ba", None), P("slab", None), P("slab", None)),
        out_specs=(P(("slab", "aa"), None), P("slab", None, "aa", "ba")),
        check_vma=False,
    )
```

```python
import jax
import jax.numpy as jnp
from jax import lax
from jax.experimental import pallas as pl
from jax.experimental.pallas import tpu as pltpu
from jax.sharding import PartitionSpec as P

ITERS = 2
F32 = jnp.float32
BF16 = jnp.bfloat16
HIGHEST = lax.Precision.HIGHEST
MIB = 1 << 20
X_PARTS = (16,) * 8
R_PARTS = (4,) * 8
LANES = 128
PAIRS = ((0, 0), (1, 0), (1, 1))


def split(value):
    high = value.astype(BF16)
    return high, (value - high.astype(F32)).astype(BF16)


def nt_dot(left, right):
    return lax.dot_general(left, right, (((1,), (1,)), ((), ())), preferred_element_type=F32)


def tn_dot(left, right):
    return lax.dot_general(left, right, (((0,), (0,)), ((), ())), preferred_element_type=F32)


def in_hbm(*values):
    return [pltpu.with_memory_space_constraint(value, pltpu.HBM) for value in values]


def call(name, kernel, grid, in_specs, out_specs, out_shape, scratch=(), vmem=16, aliases={}):
    return pl.pallas_call(
        kernel,
        name=name,
        grid_spec=pltpu.PrefetchScalarGridSpec(
            num_scalar_prefetch=1, grid=grid, in_specs=in_specs, out_specs=out_specs, scratch_shapes=list(scratch)
        ),
        out_shape=out_shape,
        input_output_aliases=aliases,
        compiler_params=pltpu.CompilerParams(vmem_limit_bytes=vmem * MIB, dimension_semantics=("arbitrary",) * len(grid)),
        cost_estimate=pl.CostEstimate(flops=0, bytes_accessed=0, transcendentals=0),
    )


def project_kernel(parts, skip, place, own_ref, other_ref, basis_ref, *rest):
    outs, basis_split = rest[skip:-1], rest[-1]
    keeps, sends = outs[: len(parts)], outs[len(parts) :]
    rank = basis_ref.shape[0]

    @pl.when(pl.program_id(0) == 0)
    def _():
        high, low = split(basis_ref[...])
        basis_split[0:rank, :] = high
        basis_split[rank:, :] = low

    first = place[0] == 0
    stacked = basis_split[...]
    for i in range(own_ref.shape[1]):
        high, low = split(jnp.concatenate([own_ref[0, i], other_ref[i]], axis=0))
        both = jnp.dot(stacked, high, preferred_element_type=F32)
        out = both[:rank] + (both[rank:] + jnp.dot(stacked[:rank], low, preferred_element_type=F32))
        left, right = out[:, :LANES], out[:, LANES:]
        keep, send = jnp.where(first, left, right), jnp.where(first, right, left)
        at = 0
        for a in range(4):
            for part, rows in enumerate(parts):
                keeps[part][a, :, i, :] = keep[at : at + rows]
                sends[part][a, :, i, :] = send[at : at + rows]
                at += rows


def project(place, field, other, basis, job, offset, total, before):
    species, x_start, xs, parts = job
    _, ys, zs = other.shape
    rank = basis.shape[0]
    block = 8
    steps = xs // block
    shapes = [(4, rows, total, zs // 2) for rows in parts] * 2
    first = x_start // block if total > xs else 0
    array = pltpu.HBM if total > xs else jax.ShapeDtypeStruct
    in_specs = [
        pl.BlockSpec((1, block, ys, zs), lambda i, place: (2 * place[1] + species, x_start // block + i, 0, 0)),
        pl.BlockSpec((block, ys, zs), lambda i, place: (offset // block + i, 0, 0)),
        pl.BlockSpec(basis.shape, lambda i, place: (0, 0)),
    ] + [pl.BlockSpec(memory_space=pl.ANY)] * len(before)
    out_specs = [pl.BlockSpec((4, s[1], block, s[3]), lambda i, place: (0, 0, first + i, 0)) for s in shapes]
    result = call(
        "project_k",
        lambda place, *refs: project_kernel(parts, len(before), place, *refs),
        (steps,),
        in_specs,
        out_specs,
        [array(s, F32) for s in shapes],
        [pltpu.VMEM((2 * rank, 2 * ys), BF16)],
        vmem=18,
        aliases={4 + index: index for index in range(len(before))},
    )(place, field, other, basis, *in_hbm(*before))
    count = len(parts)
    return result[:count], result[count:]


def add_kernel(place, keep_ref, recv_ref, *outs):
    for d in range(4):
        to = lax.bitwise_xor(place[2], d)
        outs[d][...] = keep_ref[to] + recv_ref[to]


def add_up(place, keep, recv):
    _, rows, xs, zs = keep.shape
    block = min(rows, max(1, 4 * LANES // xs))
    while rows % block:
        block -= 1
    spec = pl.BlockSpec((4, block, xs, zs), lambda i, place: (0, i, 0, 0))
    out = pl.BlockSpec((block, xs, zs), lambda i, place: (i, 0, 0))
    return call(
        "add_k",
        add_kernel,
        (rows // block,),
        [spec, spec],
        [out] * 4,
        [jax.ShapeDtypeStruct((rows, xs, zs), F32)] * 4,
        vmem=12,
    )(place, keep, recv)


def gram_kernel(parts, place, start_ref, *rest):
    lines, (out_ref, high_ref, low_ref) = rest[: 4 * parts], rest[4 * parts :]
    rows = lines[0].shape[0]
    xs = high_ref.shape[0] // 4

    @pl.when(pl.program_id(0) == 0)
    def _():
        out_ref[...] = start_ref[...]

    for d in range(4):
        base = pl.multiple_of(lax.bitwise_xor(place[2], d) * xs, xs)
        for r in range(rows):
            block = jnp.concatenate([lines[d * parts + p][r] for p in range(parts)], axis=0)
            high, low = split(block)
            high_ref[pl.ds(base, xs), r * LANES : (r + 1) * LANES] = high
            low_ref[pl.ds(base, xs), r * LANES : (r + 1) * LANES] = low
    size = out_ref.shape[1]
    for index, (i, j) in enumerate(PAIRS):
        hi, li = high_ref[i * size : (i + 1) * size], low_ref[i * size : (i + 1) * size]
        hj, lj = high_ref[j * size : (j + 1) * size], low_ref[j * size : (j + 1) * size]
        out_ref[index * size : (index + 1) * size, :] += nt_dot(hi, hj) + (nt_dot(hi, lj) + nt_dot(li, hj))


def add_gram(place, start, lines):
    parts = len(lines[0])
    rows, _, zs = lines[0][0].shape
    block = min(8, rows)
    total = 2 * start.shape[1]
    flat = [piece for group in lines for piece in group]
    whole = pl.BlockSpec(start.shape, lambda i, place: (0, 0))
    return call(
        "gram_k",
        lambda place, *refs: gram_kernel(parts, place, *refs),
        (rows // block,),
        [whole] + [pl.BlockSpec((block, *piece.shape[1:]), lambda i, place: (i, 0, 0)) for piece in flat],
        whole,
        jax.ShapeDtypeStruct(start.shape, F32),
        [pltpu.VMEM((total, block * zs), BF16)] * 2,
        vmem=20,
    )(place, start, *in_hbm(*flat))


def inverse_factor(small):
    n = small.shape[0]
    shape = (8, n)
    rows = lax.broadcasted_iota(jnp.int32, (n, n), 0)
    cols = lax.broadcasted_iota(jnp.int32, (n, n), 1)
    unit = jnp.where(rows == cols, 1.0, 0.0).astype(F32)
    tiles = [small[t : t + 8] for t in range(0, n, 8)]
    units = [unit[t : t + 8] for t in range(0, n, 8)]
    sub = lax.broadcasted_iota(jnp.int32, shape, 0)
    along_row = lambda tile, j: jnp.broadcast_to(tile[:, j : j + 1], shape)
    spread = lambda tile, i: jnp.broadcast_to(tile[i : i + 1], shape)
    done = []
    for b in range(n // 8):
        columns = [along_row(tiles[b], 8 * b + k) for k in range(8)]
        entry = [[spread(columns[k], i) if i >= k else None for k in range(8)] for i in range(8)]
        row = [spread(tiles[b], i) for i in range(8)]
        unit_row = [spread(units[b], i) for i in range(8)]
        inverse, factor = [None] * 8, [[None] * 8 for _ in range(8)]
        for k in range(8):
            inverse[k] = 1.0 / entry[k][k]
            for i in range(k + 1, 8):
                factor[i][k] = entry[i][k] * inverse[k]
                for j in range(k + 1, i + 1):
                    entry[i][j] = entry[i][j] - factor[i][k] * entry[j][k]
                row[i] = row[i] - factor[i][k] * row[k]
                unit_row[i] = unit_row[i] - factor[i][k] * unit_row[k]
        result = jnp.zeros(shape, F32)
        for k in range(8):
            result = jnp.where(sub == k, unit_row[k] * lax.rsqrt(entry[k][k]), result)
        done.append(result)
        for t in range(b + 1, n // 8):
            column = [along_row(tiles[t], 8 * b + k) for k in range(8)]
            for k in range(8):
                for m in range(k):
                    column[k] = column[k] - factor[k][m] * column[m]
                scaled = column[k] * inverse[k]
                tiles[t] = tiles[t] - scaled * row[k]
                units[t] = units[t] - scaled * unit_row[k]
    return jnp.concatenate(done, axis=0)


def basis_kernel(place, pieces_ref, start_ref, out_ref, gram_ref):
    count, size = pieces_ref.shape[0], pieces_ref.shape[1]
    for core in range(2):
        for chip in range(2):
            for d in range(4):
                at = (
                    lax.rem(place[1] + core, 2) * 8
                    + lax.rem(place[0] + chip, 2) * 4
                    + lax.bitwise_xor(place[2], d)
                )
                gram_ref[pl.ds(pl.multiple_of(at * size, 8), size), :] = pieces_ref[(core * 2 + chip) * 4 + d]
    half = gram_ref.shape[1]
    g00, g10, g11 = (gram_ref[i * half : (i + 1) * half, :] for i in range(3))
    g01 = g10.T
    dot = lambda a, b: jnp.dot(a, b, precision=HIGHEST, preferred_element_type=F32)
    out_ref[...] = start_ref[...]

    def iterate(_, carry):
        top, low = out_ref[:half], out_ref[half:]
        images = jnp.concatenate([dot(g00, top) + dot(g01, low), dot(g10, top) + dot(g11, low)], axis=0)
        small = dot(images.T, images)
        out_ref[...] = dot(images, inverse_factor(small).T)
        return carry

    lax.fori_loop(0, ITERS, iterate, 0)


def subspace(place, pieces, start):
    count, size, width = pieces.shape
    return call(
        "subspace_k",
        basis_kernel,
        (1,),
        [
            pl.BlockSpec(pieces.shape, lambda i, place: (0, 0, 0)),
            pl.BlockSpec(start.shape, lambda i, place: (0, 0)),
        ],
        pl.BlockSpec(start.shape, lambda i, place: (0, 0)),
        jax.ShapeDtypeStruct(start.shape, F32),
        [pltpu.VMEM((count * size, width), F32)],
        vmem=12,
    )(place, pieces, start)


def core_kernel(counts, steps, place, basis_ref, *rest):
    lines, (keep_ref, send_ref, factor_ref) = rest[: sum(counts)], rest[-3:]
    rank = basis_ref.shape[1]
    xs = basis_ref.shape[0] // 4

    @pl.when(pl.program_id(0) == 0)
    def _():
        for d in range(4):
            base = pl.multiple_of(lax.bitwise_xor(place[2], d) * xs, xs)
            high, low = split(basis_ref[pl.ds(base, xs), :])
            factor_ref[d * xs : (d + 1) * xs, 0:rank] = high
            factor_ref[d * xs : (d + 1) * xs, rank:] = low

    factor = factor_ref[...]

    def work(groups):
        lines = [
            jnp.concatenate([piece[r] for piece in pieces], axis=0) for pieces in groups for r in range(pieces[0].shape[0])
        ]
        high, low = split(jnp.concatenate(lines, axis=1))
        both = tn_dot(high, factor)
        out = both[:, :rank] + (both[:, rank:] + tn_dot(low, factor[:, :rank]))
        out = out.reshape(len(lines), 2, LANES // 2, rank)
        first = place[1] == 0
        keep_ref[0] = jnp.where(first, out[:, 0], out[:, 1])
        send_ref[...] = jnp.where(first, out[:, 1], out[:, 0])

    groups, at = [], 0
    for count in counts:
        groups.append(lines[at : at + count])
        at += count
    if steps is None:
        work(groups)
    else:
        for step, members in enumerate(steps):

            @pl.when(pl.program_id(0) == step)
            def _(members=members):
                work([groups[member] for member in members])


def core_of(place, basis, lines, species, whole):
    block = 8
    rank = basis.shape[1]
    groups = [[piece for d in group for piece in d] for group in lines]
    flat = [piece for group in groups for piece in group]
    rows = [group[0].shape[0] for group in groups]
    total, zs = sum(rows), flat[0].shape[2]
    before = [] if whole is None else [whole]
    if len(groups) == 1:
        steps = None
        specs = [pl.BlockSpec((block, *piece.shape[1:]), lambda i, place: (i, 0, 0)) for piece in flat]
    else:
        steps, at = [[] for _ in range(total // block)], 0
        for member, count in enumerate(rows):
            steps[at // block].append(member)
            at += count
        specs = [pl.BlockSpec(piece.shape, lambda i, place: (0, 0, 0)) for piece in flat]
    return call(
        "core_k",
        lambda place, *refs: core_kernel([len(group) for group in groups], steps, place, *refs),
        (total // block,),
        [pl.BlockSpec(basis.shape, lambda i, place: (0, 0))] + specs + [pl.BlockSpec(memory_space=pl.ANY)] * len(before),
        [
            pl.BlockSpec((1, block, zs // 2, rank), lambda i, place: (2 * place[1] + species, i, 0, 0)),
            pl.BlockSpec((block, zs // 2, rank), lambda i, place: (i, 0, 0)),
        ],
        [pltpu.HBM((4, total, zs // 2, rank), F32), pltpu.HBM((total, zs // 2, rank), F32)],
        [pltpu.VMEM((basis.shape[0], 2 * rank), BF16)],
        vmem=36,
        aliases={2 + len(flat): 0} if before else {},
    )(place, basis, *in_hbm(*flat, *before))


def finish_kernel(place, whole_ref, *refs):
    out_ref = refs[-1]
    for species, ref in enumerate(refs[:-1]):
        out_ref[species] = ref[...]


def finish(place, whole, came):
    rows, zs, rank = came[0].shape
    block = 8
    return call(
        "finish_k",
        finish_kernel,
        (rows // block,),
        [pl.BlockSpec(memory_space=pl.ANY)] + [pl.BlockSpec((block, zs, rank), lambda i, place: (i, 0, 0))] * 2,
        pl.BlockSpec((2, block, zs, rank), lambda i, place: (1 - place[1], i, 0, 0)),
        pltpu.HBM(whole.shape, F32),
        aliases={1: 0},
    )(place, *in_hbm(whole), *came)


def after(value, *earlier):
    return lax.optimization_barrier((value, *earlier))[0]


def pair_swap(value, distance):
    return lax.ppermute(value, "ba", [(i, i ^ distance) for i in range(4)])


def z_swap(value, d):
    return lax.ppermute(value, "aa", [(i, i ^ d) for i in range(4)])


def reduce_gram(place, gram):
    chip, core, z = place[0], place[1], place[2]
    rows, width = gram.shape
    halves = gram.reshape(2, rows // 2, width)
    take = lambda array, i: lax.dynamic_index_in_dim(array, i, 0, keepdims=False)
    gram = take(halves, core) + pair_swap(take(halves, 1 - core), 1)
    halves = gram.reshape(2, rows // 4, width)
    gram = take(halves, chip) + pair_swap(take(halves, 1 - chip), 2)
    blocks = gram.reshape(4, rows // 16, width)
    came = [z_swap(take(blocks, z ^ d), d) for d in (1, 2, 3)]
    gram = take(blocks, z) + came[0] + came[1] + came[2]
    gram = jnp.stack([gram] + [z_swap(gram, d) for d in (1, 2, 3)])
    gram = jnp.concatenate([gram, pair_swap(gram, 2)])
    return jnp.concatenate([gram, pair_swap(gram, 1)])


def fast_body(slab_field, x_basis, y_basis):
    rank = x_basis.shape[1]
    species, xs, ys, zs = slab_field.shape
    ba = lax.axis_index("ba")
    chip, core, z = ba // 2, ba % 2, lax.axis_index("aa")
    place = jnp.stack([chip, core, z]).astype(jnp.int32)
    rows = lambda index: lax.dynamic_slice_in_dim(y_basis, index * ys, ys, 0)
    basis_t = jnp.concatenate([rows(ba), rows(ba ^ 1)], axis=0).T

    share = rank // 4
    jobs, at = [], 0
    for size in X_PARTS:
        jobs.append((0, at, size, (share,)))
        at += size
    late = [(1, start, xs // 2, R_PARTS) for start in (0, xs // 2)]
    jobs[3:3] = late
    keeps, sends, came, lines = [], [], [], []
    halves = []
    grams = [jnp.zeros((len(PAIRS) * xs * 2, xs * 2), F32)]
    count = len(X_PARTS)

    def spread(i):
        mine = add_up(place, keeps[i], came[i])
        line = [mine[0], None, None, None]
        for d, earlier in ((2, 1), (3, 2), (1, 3)):
            ready = [lines[-1][earlier]] if lines else []
            if i + 1 == len(X_PARTS) + len(R_PARTS) and d == 1:
                ready.append(grams[-2])
            part = after(mine[d], *ready)
            line[d] = z_swap(part, d)
        lines.append(line)
        if i >= count - 1:
            group = [[old[d] for old in lines[:count]] for d in range(4)] if i == count - 1 else [[part] for part in line]
            grams.append(add_gram(place, grams[-1], group))

    def exchange(part):
        i = len(came)
        earlier = []
        if i >= 2:
            earlier = [came[i - 2]] + (lines[i - 3][1:] if i >= 3 else [])
        if i in (6, 7):
            earlier.append(halves[i - 6])
        if i >= count + 3:
            earlier.append(grams[i - count - 2])
        came.append(pair_swap(after(part, *earlier), 2))
        if i >= 1:
            spread(i - 1)

    swaps = [(0, 0, X_PARTS[0]), (0, X_PARTS[0], xs - X_PARTS[0]), (1, 0, xs)]
    others, theirs, second = [], [], []
    for job in jobs:
        while swaps and swaps[0][0] <= job[0] and swaps[0][1] <= job[1]:
            s, start, size = swaps.pop(0)
            earlier = ([], sends[:1], lines[0][:1] if lines else [])[len(theirs)]
            first = after(2 * (1 - core) + s, *earlier)
            theirs.append(lax.dynamic_slice(slab_field, (first, start, 0, 0), (1, size, ys, zs))[0])
            others.append((s, start, pair_swap(theirs[-1], 1)))
        base, other = [(start, array) for s, start, array in others if s == job[0] and start <= job[1]][-1]
        if job[0] == 0:
            keep, send = project(place, slab_field, other, basis_t, job, job[1] - base, job[2], [])
        else:
            keep, send = project(place, slab_field, other, basis_t, job, job[1] - base, xs, second)
            second = [*keep, *send]
            halves.append(send[0])
            continue
        for mine, part in zip(keep, send):
            keeps.append(mine)
            sends.append(part)
            exchange(part)
    for mine, part in zip(second[: len(R_PARTS)], second[len(R_PARTS) :]):
        keeps.append(mine)
        sends.append(part)
        exchange(part)
    spread(len(keeps) - 1)

    first = [[line[d] for line in lines[:count]] for d in range(4)]
    second = [[[line[d]] for d in range(4)] for line in lines[count:]]
    basis = subspace(place, reduce_gram(place, grams[-1]), x_basis)

    whole, send0 = core_of(place, basis, [first], 0, None)
    came0 = pair_swap(send0, 1)
    whole, send1 = core_of(place, basis, second, 1, whole)
    core_tensor = finish(place, whole, [came0, pair_swap(send1, 1)]).transpose(0, 3, 1, 2)
    new_basis = lax.dynamic_slice_in_dim(basis, z * xs, xs, 0)
    return new_basis, core_tensor


def orthonormal(images):
    small = jnp.dot(images.T, images, precision=HIGHEST)
    lower = jnp.linalg.cholesky(small)
    return lax.linalg.triangular_solve(lower, images, left_side=False, lower=True, transpose_a=True)


def plain_body(slab_field, x_basis, y_basis):
    y_rows = slab_field.shape[2]
    local_basis = lax.dynamic_slice_in_dim(y_basis, lax.axis_index("ba") * y_rows, y_rows, 0)
    partial_value = jnp.einsum("sxyz,yr->sxrz", slab_field, local_basis, precision=HIGHEST)
    projected = lax.psum_scatter(partial_value, "ba", scatter_dimension=3, tiled=True)
    columns = lax.all_to_all(projected, "aa", split_axis=2, concat_axis=1, tiled=True)
    basis = x_basis
    local_gram = jnp.einsum("sxrz,svrz->xv", columns, columns, precision=HIGHEST)
    gram_matrix = lax.psum(local_gram, ("aa", "ba"))
    for _ in range(ITERS):
        basis = orthonormal(jnp.dot(gram_matrix, basis, precision=HIGHEST))
    core_tensor = jnp.einsum("xk,sxrz->skrz", basis, columns, precision=HIGHEST)
    basis_rows = x_basis.shape[0] // lax.axis_size("aa")
    new_basis = lax.dynamic_slice_in_dim(basis, lax.axis_index("aa") * basis_rows, basis_rows, 0)
    return new_basis, core_tensor


def solution(mesh):
    def body(slab_field, x_basis, y_basis):
        fits = (
            mesh.shape["aa"] == 4
            and mesh.shape["ba"] == 4
            and slab_field.shape == (4, LANES, LANES, 2 * LANES)
            and x_basis.shape == y_basis.shape == (4 * LANES, LANES)
        )
        return (fast_body if fits else plain_body)(slab_field, x_basis, y_basis)

    return jax.shard_map(
        body,
        mesh=mesh,
        in_specs=(P("slab", "aa", "ba", None), P("slab", None), P("slab", None)),
        out_specs=(P(("slab", "aa"), None), P("slab", None, "aa", "ba")),
        check_vma=False,
    )
```

```python
import jax
import jax.numpy as jnp
from jax import lax
from jax.experimental import pallas as pl
from jax.experimental.pallas import tpu as pltpu
from jax.sharding import PartitionSpec as P

ITERS = 2
F32 = jnp.float32
BF16 = jnp.bfloat16
HIGHEST = lax.Precision.HIGHEST
MIB = 1 << 20
X_PARTS = (16,) * 8
R_PARTS = (4,) * 7 + (2, 2)
LANES = 128
PAIRS = ((0, 0), (1, 0), (1, 1))


def split(value):
    high = value.astype(BF16)
    return high, (value - high.astype(F32)).astype(BF16)


def nt_dot(left, right):
    return lax.dot_general(left, right, (((1,), (1,)), ((), ())), preferred_element_type=F32)


def tn_dot(left, right):
    return lax.dot_general(left, right, (((0,), (0,)), ((), ())), preferred_element_type=F32)


def in_hbm(*values):
    return [pltpu.with_memory_space_constraint(value, pltpu.HBM) for value in values]


def call(name, kernel, grid, in_specs, out_specs, out_shape, scratch=(), vmem=16, aliases={}):
    return pl.pallas_call(
        kernel,
        name=name,
        grid_spec=pltpu.PrefetchScalarGridSpec(
            num_scalar_prefetch=1, grid=grid, in_specs=in_specs, out_specs=out_specs, scratch_shapes=list(scratch)
        ),
        out_shape=out_shape,
        input_output_aliases=aliases,
        compiler_params=pltpu.CompilerParams(vmem_limit_bytes=vmem * MIB, dimension_semantics=("arbitrary",) * len(grid)),
        cost_estimate=pl.CostEstimate(flops=0, bytes_accessed=0, transcendentals=0),
    )


def project_kernel(parts, skip, place, own_ref, other_ref, basis_ref, *rest):
    outs, basis_split = rest[skip:-1], rest[-1]
    keeps, sends = outs[: len(parts)], outs[len(parts) :]
    rank = basis_ref.shape[0]

    @pl.when(pl.program_id(0) == 0)
    def _():
        high, low = split(basis_ref[...])
        basis_split[0:rank, :] = high
        basis_split[rank:, :] = low

    first = place[0] == 0
    stacked = basis_split[...]
    for i in range(own_ref.shape[1]):
        high, low = split(jnp.concatenate([own_ref[0, i], other_ref[i]], axis=0))
        both = jnp.dot(stacked, high, preferred_element_type=F32)
        out = both[:rank] + (both[rank:] + jnp.dot(stacked[:rank], low, preferred_element_type=F32))
        left, right = out[:, :LANES], out[:, LANES:]
        keep, send = jnp.where(first, left, right), jnp.where(first, right, left)
        at = 0
        for a in range(4):
            for part, rows in enumerate(parts):
                keeps[part][a, :, i, :] = keep[at : at + rows]
                sends[part][a, :, i, :] = send[at : at + rows]
                at += rows


def project(place, field, other, basis, job, offset, total, before):
    species, x_start, xs, parts = job
    _, ys, zs = other.shape
    rank = basis.shape[0]
    block = 8
    steps = xs // block
    shapes = [(4, rows, total, zs // 2) for rows in parts] * 2
    first = x_start // block if total > xs else 0
    array = pltpu.HBM if total > xs else jax.ShapeDtypeStruct
    in_specs = [
        pl.BlockSpec((1, block, ys, zs), lambda i, place: (2 * place[1] + species, x_start // block + i, 0, 0)),
        pl.BlockSpec((block, ys, zs), lambda i, place: (offset // block + i, 0, 0)),
        pl.BlockSpec(basis.shape, lambda i, place: (0, 0)),
    ] + [pl.BlockSpec(memory_space=pl.ANY)] * len(before)
    out_specs = [pl.BlockSpec((4, s[1], block, s[3]), lambda i, place: (0, 0, first + i, 0)) for s in shapes]
    result = call(
        "project_k",
        lambda place, *refs: project_kernel(parts, len(before), place, *refs),
        (steps,),
        in_specs,
        out_specs,
        [array(s, F32) for s in shapes],
        [pltpu.VMEM((2 * rank, 2 * ys), BF16)],
        vmem=18,
        aliases={4 + index: index for index in range(len(before))},
    )(place, field, other, basis, *in_hbm(*before))
    count = len(parts)
    return result[:count], result[count:]


def add_kernel(place, keep_ref, recv_ref, *outs):
    for d in range(4):
        to = lax.bitwise_xor(place[2], d)
        outs[d][...] = keep_ref[to] + recv_ref[to]


def add_up(place, keep, recv):
    _, rows, xs, zs = keep.shape
    block = min(rows, max(1, 4 * LANES // xs))
    while rows % block:
        block -= 1
    spec = pl.BlockSpec((4, block, xs, zs), lambda i, place: (0, i, 0, 0))
    out = pl.BlockSpec((block, xs, zs), lambda i, place: (i, 0, 0))
    return call(
        "add_k",
        add_kernel,
        (rows // block,),
        [spec, spec],
        [out] * 4,
        [jax.ShapeDtypeStruct((rows, xs, zs), F32)] * 4,
        vmem=12,
    )(place, keep, recv)


def gram_kernel(parts, place, start_ref, *rest):
    lines, (out_ref, high_ref, low_ref) = rest[: 4 * parts], rest[4 * parts :]
    rows = lines[0].shape[0]
    xs = high_ref.shape[0] // 4

    @pl.when(pl.program_id(0) == 0)
    def _():
        out_ref[...] = start_ref[...]

    for d in range(4):
        base = pl.multiple_of(lax.bitwise_xor(place[2], d) * xs, xs)
        for r in range(rows):
            block = jnp.concatenate([lines[d * parts + p][r] for p in range(parts)], axis=0)
            high, low = split(block)
            high_ref[pl.ds(base, xs), r * LANES : (r + 1) * LANES] = high
            low_ref[pl.ds(base, xs), r * LANES : (r + 1) * LANES] = low
    size = out_ref.shape[1]
    for index, (i, j) in enumerate(PAIRS):
        hi, li = high_ref[i * size : (i + 1) * size], low_ref[i * size : (i + 1) * size]
        hj, lj = high_ref[j * size : (j + 1) * size], low_ref[j * size : (j + 1) * size]
        out_ref[index * size : (index + 1) * size, :] += nt_dot(hi, hj) + (nt_dot(hi, lj) + nt_dot(li, hj))


def add_gram(place, start, lines):
    parts = len(lines[0])
    rows, _, zs = lines[0][0].shape
    block = min(8, rows)
    total = 2 * start.shape[1]
    flat = [piece for group in lines for piece in group]
    whole = pl.BlockSpec(start.shape, lambda i, place: (0, 0))
    return call(
        "gram_k",
        lambda place, *refs: gram_kernel(parts, place, *refs),
        (rows // block,),
        [whole] + [pl.BlockSpec((block, *piece.shape[1:]), lambda i, place: (i, 0, 0)) for piece in flat],
        whole,
        jax.ShapeDtypeStruct(start.shape, F32),
        [pltpu.VMEM((total, block * zs), BF16)] * 2,
        vmem=20,
    )(place, start, *in_hbm(*flat))


def inverse_factor(small):
    n = small.shape[0]
    shape = (8, n)
    rows = lax.broadcasted_iota(jnp.int32, (n, n), 0)
    cols = lax.broadcasted_iota(jnp.int32, (n, n), 1)
    unit = jnp.where(rows == cols, 1.0, 0.0).astype(F32)
    tiles = [small[t : t + 8] for t in range(0, n, 8)]
    units = [unit[t : t + 8] for t in range(0, n, 8)]
    sub = lax.broadcasted_iota(jnp.int32, shape, 0)
    along_row = lambda tile, j: jnp.broadcast_to(tile[:, j : j + 1], shape)
    spread = lambda tile, i: jnp.broadcast_to(tile[i : i + 1], shape)
    done = []
    for b in range(n // 8):
        columns = [along_row(tiles[b], 8 * b + k) for k in range(8)]
        entry = [[spread(columns[k], i) if i >= k else None for k in range(8)] for i in range(8)]
        row = [spread(tiles[b], i) for i in range(8)]
        unit_row = [spread(units[b], i) for i in range(8)]
        inverse, factor = [None] * 8, [[None] * 8 for _ in range(8)]
        for k in range(8):
            inverse[k] = 1.0 / entry[k][k]
            for i in range(k + 1, 8):
                factor[i][k] = entry[i][k] * inverse[k]
                for j in range(k + 1, i + 1):
                    entry[i][j] = entry[i][j] - factor[i][k] * entry[j][k]
                row[i] = row[i] - factor[i][k] * row[k]
                unit_row[i] = unit_row[i] - factor[i][k] * unit_row[k]
        result = jnp.zeros(shape, F32)
        for k in range(8):
            result = jnp.where(sub == k, unit_row[k] * lax.rsqrt(entry[k][k]), result)
        done.append(result)
        for t in range(b + 1, n // 8):
            column = [along_row(tiles[t], 8 * b + k) for k in range(8)]
            for k in range(8):
                for m in range(k):
                    column[k] = column[k] - factor[k][m] * column[m]
                scaled = column[k] * inverse[k]
                tiles[t] = tiles[t] - scaled * row[k]
                units[t] = units[t] - scaled * unit_row[k]
    return jnp.concatenate(done, axis=0)


def basis_kernel(place, pieces_ref, start_ref, out_ref, gram_ref):
    count, size = pieces_ref.shape[0], pieces_ref.shape[1]
    for core in range(2):
        for chip in range(2):
            for d in range(4):
                at = (
                    lax.rem(place[1] + core, 2) * 8
                    + lax.rem(place[0] + chip, 2) * 4
                    + lax.bitwise_xor(place[2], d)
                )
                gram_ref[pl.ds(pl.multiple_of(at * size, 8), size), :] = pieces_ref[(core * 2 + chip) * 4 + d]
    half = gram_ref.shape[1]
    g00, g10, g11 = (gram_ref[i * half : (i + 1) * half, :] for i in range(3))
    g01 = g10.T
    dot = lambda a, b: jnp.dot(a, b, precision=HIGHEST, preferred_element_type=F32)
    out_ref[...] = start_ref[...]

    def iterate(_, carry):
        top, low = out_ref[:half], out_ref[half:]
        images = jnp.concatenate([dot(g00, top) + dot(g01, low), dot(g10, top) + dot(g11, low)], axis=0)
        small = dot(images.T, images)
        out_ref[...] = dot(images, inverse_factor(small).T)
        return carry

    lax.fori_loop(0, ITERS, iterate, 0)


def subspace(place, pieces, start):
    count, size, width = pieces.shape
    return call(
        "subspace_k",
        basis_kernel,
        (1,),
        [
            pl.BlockSpec(pieces.shape, lambda i, place: (0, 0, 0)),
            pl.BlockSpec(start.shape, lambda i, place: (0, 0)),
        ],
        pl.BlockSpec(start.shape, lambda i, place: (0, 0)),
        jax.ShapeDtypeStruct(start.shape, F32),
        [pltpu.VMEM((count * size, width), F32)],
        vmem=12,
    )(place, pieces, start)


def core_kernel(counts, steps, place, basis_ref, *rest):
    lines, (keep_ref, send_ref, factor_ref) = rest[: sum(counts)], rest[-3:]
    rank = basis_ref.shape[1]
    xs = basis_ref.shape[0] // 4

    @pl.when(pl.program_id(0) == 0)
    def _():
        for d in range(4):
            base = pl.multiple_of(lax.bitwise_xor(place[2], d) * xs, xs)
            high, low = split(basis_ref[pl.ds(base, xs), :])
            factor_ref[d * xs : (d + 1) * xs, 0:rank] = high
            factor_ref[d * xs : (d + 1) * xs, rank:] = low

    factor = factor_ref[...]

    def work(groups):
        lines = [
            jnp.concatenate([piece[r] for piece in pieces], axis=0) for pieces in groups for r in range(pieces[0].shape[0])
        ]
        high, low = split(jnp.concatenate(lines, axis=1))
        both = tn_dot(high, factor)
        out = both[:, :rank] + (both[:, rank:] + tn_dot(low, factor[:, :rank]))
        out = out.reshape(len(lines), 2, LANES // 2, rank)
        first = place[1] == 0
        keep_ref[0] = jnp.where(first, out[:, 0], out[:, 1])
        send_ref[...] = jnp.where(first, out[:, 1], out[:, 0])

    groups, at = [], 0
    for count in counts:
        groups.append(lines[at : at + count])
        at += count
    if steps is None:
        work(groups)
    else:
        for step, members in enumerate(steps):

            @pl.when(pl.program_id(0) == step)
            def _(members=members):
                work([groups[member] for member in members])


def core_of(place, basis, lines, species, whole):
    block = 8
    rank = basis.shape[1]
    groups = [[piece for d in group for piece in d] for group in lines]
    flat = [piece for group in groups for piece in group]
    rows = [group[0].shape[0] for group in groups]
    total, zs = sum(rows), flat[0].shape[2]
    before = [] if whole is None else [whole]
    if len(groups) == 1:
        steps = None
        specs = [pl.BlockSpec((block, *piece.shape[1:]), lambda i, place: (i, 0, 0)) for piece in flat]
    else:
        steps, at = [[] for _ in range(total // block)], 0
        for member, count in enumerate(rows):
            steps[at // block].append(member)
            at += count
        specs = [pl.BlockSpec(piece.shape, lambda i, place: (0, 0, 0)) for piece in flat]
    return call(
        "core_k",
        lambda place, *refs: core_kernel([len(group) for group in groups], steps, place, *refs),
        (total // block,),
        [pl.BlockSpec(basis.shape, lambda i, place: (0, 0))] + specs + [pl.BlockSpec(memory_space=pl.ANY)] * len(before),
        [
            pl.BlockSpec((1, block, zs // 2, rank), lambda i, place: (2 * place[1] + species, i, 0, 0)),
            pl.BlockSpec((block, zs // 2, rank), lambda i, place: (i, 0, 0)),
        ],
        [pltpu.HBM((4, total, zs // 2, rank), F32), pltpu.HBM((total, zs // 2, rank), F32)],
        [pltpu.VMEM((basis.shape[0], 2 * rank), BF16)],
        vmem=36,
        aliases={2 + len(flat): 0} if before else {},
    )(place, basis, *in_hbm(*flat, *before))


def finish_kernel(place, whole_ref, *refs):
    out_ref = refs[-1]
    for species, ref in enumerate(refs[:-1]):
        out_ref[species] = ref[...]


def finish(place, whole, came):
    rows, zs, rank = came[0].shape
    block = 8
    return call(
        "finish_k",
        finish_kernel,
        (rows // block,),
        [pl.BlockSpec(memory_space=pl.ANY)] + [pl.BlockSpec((block, zs, rank), lambda i, place: (i, 0, 0))] * 2,
        pl.BlockSpec((2, block, zs, rank), lambda i, place: (1 - place[1], i, 0, 0)),
        pltpu.HBM(whole.shape, F32),
        aliases={1: 0},
    )(place, *in_hbm(whole), *came)


def after(value, *earlier):
    return lax.optimization_barrier((value, *earlier))[0]


def pair_swap(value, distance):
    return lax.ppermute(value, "ba", [(i, i ^ distance) for i in range(4)])


def z_swap(value, d):
    return lax.ppermute(value, "aa", [(i, i ^ d) for i in range(4)])


def reduce_gram(place, gram):
    chip, core, z = place[0], place[1], place[2]
    rows, width = gram.shape
    halves = gram.reshape(2, rows // 2, width)
    take = lambda array, i: lax.dynamic_index_in_dim(array, i, 0, keepdims=False)
    gram = take(halves, core) + pair_swap(take(halves, 1 - core), 1)
    halves = gram.reshape(2, rows // 4, width)
    gram = take(halves, chip) + pair_swap(take(halves, 1 - chip), 2)
    blocks = gram.reshape(4, rows // 16, width)
    came = [z_swap(take(blocks, z ^ d), d) for d in (1, 2, 3)]
    gram = take(blocks, z) + came[0] + came[1] + came[2]
    gram = jnp.stack([gram] + [z_swap(gram, d) for d in (1, 2, 3)])
    gram = jnp.concatenate([gram, pair_swap(gram, 2)])
    return jnp.concatenate([gram, pair_swap(gram, 1)])


def fast_body(slab_field, x_basis, y_basis):
    rank = x_basis.shape[1]
    species, xs, ys, zs = slab_field.shape
    ba = lax.axis_index("ba")
    chip, core, z = ba // 2, ba % 2, lax.axis_index("aa")
    place = jnp.stack([chip, core, z]).astype(jnp.int32)
    rows = lambda index: lax.dynamic_slice_in_dim(y_basis, index * ys, ys, 0)
    basis_t = jnp.concatenate([rows(ba), rows(ba ^ 1)], axis=0).T

    share = rank // 4
    jobs, at = [], 0
    for size in X_PARTS:
        jobs.append((0, at, size, (share,)))
        at += size
    late = [(1, start, xs // 2, R_PARTS) for start in (0, xs // 2)]
    jobs[3:3] = late
    keeps, sends, came, lines = [], [], [], []
    halves = []
    grams = [jnp.zeros((len(PAIRS) * xs * 2, xs * 2), F32)]
    count = len(X_PARTS)

    def spread(i):
        mine = add_up(place, keeps[i], came[i])
        line = [mine[0], None, None, None]
        for d, earlier in ((2, 1), (3, 2), (1, 3)):
            ready = [lines[-1][earlier]] if lines else []
            if i + 1 == len(X_PARTS) + len(R_PARTS) and d == 1:
                ready.append(grams[-2])
            part = after(mine[d], *ready)
            line[d] = z_swap(part, d)
        lines.append(line)
        if i >= count - 1:
            group = [[old[d] for old in lines[:count]] for d in range(4)] if i == count - 1 else [[part] for part in line]
            grams.append(add_gram(place, grams[-1], group))

    def exchange(part):
        i = len(came)
        earlier = []
        if i >= 2:
            earlier = [came[i - 2]] + (lines[i - 3][1:] if i >= 3 else [])
        if i in (6, 7):
            earlier.append(halves[i - 6])
        if i >= count + 3:
            earlier.append(grams[i - count - 2])
        came.append(pair_swap(after(part, *earlier), 2))
        if i >= 1:
            spread(i - 1)

    swaps = [(0, 0, X_PARTS[0]), (0, X_PARTS[0], xs - X_PARTS[0]), (1, 0, xs)]
    others, theirs, second = [], [], []
    for job in jobs:
        while swaps and swaps[0][0] <= job[0] and swaps[0][1] <= job[1]:
            s, start, size = swaps.pop(0)
            earlier = ([], sends[:1], lines[0][:1] if lines else [])[len(theirs)]
            first = after(2 * (1 - core) + s, *earlier)
            theirs.append(lax.dynamic_slice(slab_field, (first, start, 0, 0), (1, size, ys, zs))[0])
            others.append((s, start, pair_swap(theirs[-1], 1)))
        base, other = [(start, array) for s, start, array in others if s == job[0] and start <= job[1]][-1]
        if job[0] == 0:
            keep, send = project(place, slab_field, other, basis_t, job, job[1] - base, job[2], [])
        else:
            keep, send = project(place, slab_field, other, basis_t, job, job[1] - base, xs, second)
            second = [*keep, *send]
            halves.append(send[0])
            continue
        for mine, part in zip(keep, send):
            keeps.append(mine)
            sends.append(part)
            exchange(part)
    for mine, part in zip(second[: len(R_PARTS)], second[len(R_PARTS) :]):
        keeps.append(mine)
        sends.append(part)
        exchange(part)
    spread(len(keeps) - 1)

    first = [[line[d] for line in lines[:count]] for d in range(4)]
    second = [[[line[d]] for d in range(4)] for line in lines[count:]]
    basis = subspace(place, reduce_gram(place, grams[-1]), x_basis)

    whole, send0 = core_of(place, basis, [first], 0, None)
    came0 = pair_swap(send0, 1)
    whole, send1 = core_of(place, basis, second, 1, whole)
    core_tensor = finish(place, whole, [came0, pair_swap(send1, 1)]).transpose(0, 3, 1, 2)
    new_basis = lax.dynamic_slice_in_dim(basis, z * xs, xs, 0)
    return new_basis, core_tensor


def orthonormal(images):
    small = jnp.dot(images.T, images, precision=HIGHEST)
    lower = jnp.linalg.cholesky(small)
    return lax.linalg.triangular_solve(lower, images, left_side=False, lower=True, transpose_a=True)


def plain_body(slab_field, x_basis, y_basis):
    y_rows = slab_field.shape[2]
    local_basis = lax.dynamic_slice_in_dim(y_basis, lax.axis_index("ba") * y_rows, y_rows, 0)
    partial_value = jnp.einsum("sxyz,yr->sxrz", slab_field, local_basis, precision=HIGHEST)
    projected = lax.psum_scatter(partial_value, "ba", scatter_dimension=3, tiled=True)
    columns = lax.all_to_all(projected, "aa", split_axis=2, concat_axis=1, tiled=True)
    basis = x_basis
    local_gram = jnp.einsum("sxrz,svrz->xv", columns, columns, precision=HIGHEST)
    gram_matrix = lax.psum(local_gram, ("aa", "ba"))
    for _ in range(ITERS):
        basis = orthonormal(jnp.dot(gram_matrix, basis, precision=HIGHEST))
    core_tensor = jnp.einsum("xk,sxrz->skrz", basis, columns, precision=HIGHEST)
    basis_rows = x_basis.shape[0] // lax.axis_size("aa")
    new_basis = lax.dynamic_slice_in_dim(basis, lax.axis_index("aa") * basis_rows, basis_rows, 0)
    return new_basis, core_tensor


def solution(mesh):
    def body(slab_field, x_basis, y_basis):
        fits = (
            mesh.shape["aa"] == 4
            and mesh.shape["ba"] == 4
            and slab_field.shape == (4, LANES, LANES, 2 * LANES)
            and x_basis.shape == y_basis.shape == (4 * LANES, LANES)
        )
        return (fast_body if fits else plain_body)(slab_field, x_basis, y_basis)

    return jax.shard_map(
        body,
        mesh=mesh,
        in_specs=(P("slab", "aa", "ba", None), P("slab", None), P("slab", None)),
        out_specs=(P(("slab", "aa"), None), P("slab", None, "aa", "ba")),
        check_vma=False,
    )
```

```python
import jax
import jax.numpy as jnp
from jax import lax
from jax.experimental import pallas as pl
from jax.experimental.pallas import tpu as pltpu
from jax.sharding import PartitionSpec as P

ITERS = 2
F32 = jnp.float32
BF16 = jnp.bfloat16
HIGHEST = lax.Precision.HIGHEST
MIB = 1 << 20
X_PARTS = (16,) * 8
R_PARTS = (4,) * 8
LANES = 128
PAIRS = ((0, 0), (1, 0), (1, 1))


def split(value):
    high = value.astype(BF16)
    return high, (value - high.astype(F32)).astype(BF16)


def nt_dot(left, right):
    return lax.dot_general(left, right, (((1,), (1,)), ((), ())), preferred_element_type=F32)


def tn_dot(left, right):
    return lax.dot_general(left, right, (((0,), (0,)), ((), ())), preferred_element_type=F32)


def in_hbm(*values):
    return [pltpu.with_memory_space_constraint(value, pltpu.HBM) for value in values]


def call(name, kernel, grid, in_specs, out_specs, out_shape, scratch=(), vmem=16, aliases={}):
    return pl.pallas_call(
        kernel,
        name=name,
        grid_spec=pltpu.PrefetchScalarGridSpec(
            num_scalar_prefetch=1, grid=grid, in_specs=in_specs, out_specs=out_specs, scratch_shapes=list(scratch)
        ),
        out_shape=out_shape,
        input_output_aliases=aliases,
        compiler_params=pltpu.CompilerParams(vmem_limit_bytes=vmem * MIB, dimension_semantics=("arbitrary",) * len(grid)),
        cost_estimate=pl.CostEstimate(flops=0, bytes_accessed=0, transcendentals=0),
    )


def project_kernel(parts, skip, place, own_ref, other_ref, basis_ref, *rest):
    outs, basis_split = rest[skip:-1], rest[-1]
    keeps, sends = outs[: len(parts)], outs[len(parts) :]
    rank = basis_ref.shape[0]

    @pl.when(pl.program_id(0) == 0)
    def _():
        high, low = split(basis_ref[...])
        basis_split[0:rank, :] = high
        basis_split[rank:, :] = low

    first = place[0] == 0
    stacked = basis_split[...]
    for i in range(own_ref.shape[1]):
        high, low = split(jnp.concatenate([own_ref[0, i], other_ref[i]], axis=0))
        both = jnp.dot(stacked, high, preferred_element_type=F32)
        out = both[:rank] + (both[rank:] + jnp.dot(stacked[:rank], low, preferred_element_type=F32))
        left, right = out[:, :LANES], out[:, LANES:]
        keep, send = jnp.where(first, left, right), jnp.where(first, right, left)
        at = 0
        for a in range(4):
            for part, rows in enumerate(parts):
                keeps[part][a, :, i, :] = keep[at : at + rows]
                sends[part][a, :, i, :] = send[at : at + rows]
                at += rows


def project(place, field, other, basis, job, offset, total, before):
    species, x_start, xs, parts = job
    _, ys, zs = other.shape
    rank = basis.shape[0]
    block = 8
    steps = xs // block
    shapes = [(4, rows, total, zs // 2) for rows in parts] * 2
    first = x_start // block if total > xs else 0
    array = pltpu.HBM if total > xs else jax.ShapeDtypeStruct
    in_specs = [
        pl.BlockSpec((1, block, ys, zs), lambda i, place: (2 * place[1] + species, x_start // block + i, 0, 0)),
        pl.BlockSpec((block, ys, zs), lambda i, place: (offset // block + i, 0, 0)),
        pl.BlockSpec(basis.shape, lambda i, place: (0, 0)),
    ] + [pl.BlockSpec(memory_space=pl.ANY)] * len(before)
    out_specs = [pl.BlockSpec((4, s[1], block, s[3]), lambda i, place: (0, 0, first + i, 0)) for s in shapes]
    result = call(
        "project_k",
        lambda place, *refs: project_kernel(parts, len(before), place, *refs),
        (steps,),
        in_specs,
        out_specs,
        [array(s, F32) for s in shapes],
        [pltpu.VMEM((2 * rank, 2 * ys), BF16)],
        vmem=18,
        aliases={4 + index: index for index in range(len(before))},
    )(place, field, other, basis, *in_hbm(*before))
    count = len(parts)
    return result[:count], result[count:]


def add_kernel(place, keep_ref, recv_ref, *outs):
    for d in range(4):
        to = lax.bitwise_xor(place[2], d)
        outs[d][...] = keep_ref[to] + recv_ref[to]


def add_up(place, keep, recv):
    _, rows, xs, zs = keep.shape
    block = min(rows, max(1, 4 * LANES // xs))
    while rows % block:
        block -= 1
    spec = pl.BlockSpec((4, block, xs, zs), lambda i, place: (0, i, 0, 0))
    out = pl.BlockSpec((block, xs, zs), lambda i, place: (i, 0, 0))
    return call(
        "add_k",
        add_kernel,
        (rows // block,),
        [spec, spec],
        [out] * 4,
        [jax.ShapeDtypeStruct((rows, xs, zs), F32)] * 4,
        vmem=12,
    )(place, keep, recv)


def gram_kernel(parts, place, start_ref, *rest):
    lines, (out_ref, high_ref, low_ref) = rest[: 4 * parts], rest[4 * parts :]
    rows = lines[0].shape[0]
    xs = high_ref.shape[0] // 4

    @pl.when(pl.program_id(0) == 0)
    def _():
        out_ref[...] = start_ref[...]

    for d in range(4):
        base = pl.multiple_of(lax.bitwise_xor(place[2], d) * xs, xs)
        for r in range(rows):
            block = jnp.concatenate([lines[d * parts + p][r] for p in range(parts)], axis=0)
            high, low = split(block)
            high_ref[pl.ds(base, xs), r * LANES : (r + 1) * LANES] = high
            low_ref[pl.ds(base, xs), r * LANES : (r + 1) * LANES] = low
    size = out_ref.shape[1]
    for index, (i, j) in enumerate(PAIRS):
        hi, li = high_ref[i * size : (i + 1) * size], low_ref[i * size : (i + 1) * size]
        hj, lj = high_ref[j * size : (j + 1) * size], low_ref[j * size : (j + 1) * size]
        out_ref[index * size : (index + 1) * size, :] += nt_dot(hi, hj) + (nt_dot(hi, lj) + nt_dot(li, hj))


def add_gram(place, start, lines):
    parts = len(lines[0])
    rows, _, zs = lines[0][0].shape
    block = min(8, rows)
    total = 2 * start.shape[1]
    flat = [piece for group in lines for piece in group]
    whole = pl.BlockSpec(start.shape, lambda i, place: (0, 0))
    return call(
        "gram_k",
        lambda place, *refs: gram_kernel(parts, place, *refs),
        (rows // block,),
        [whole] + [pl.BlockSpec((block, *piece.shape[1:]), lambda i, place: (i, 0, 0)) for piece in flat],
        whole,
        jax.ShapeDtypeStruct(start.shape, F32),
        [pltpu.VMEM((total, block * zs), BF16)] * 2,
        vmem=20,
    )(place, start, *in_hbm(*flat))


def inverse_factor(small):
    n = small.shape[0]
    shape = (8, n)
    rows = lax.broadcasted_iota(jnp.int32, (n, n), 0)
    cols = lax.broadcasted_iota(jnp.int32, (n, n), 1)
    unit = jnp.where(rows == cols, 1.0, 0.0).astype(F32)
    tiles = [small[t : t + 8] for t in range(0, n, 8)]
    units = [unit[t : t + 8] for t in range(0, n, 8)]
    sub = lax.broadcasted_iota(jnp.int32, shape, 0)
    along_row = lambda tile, j: jnp.broadcast_to(tile[:, j : j + 1], shape)
    spread = lambda tile, i: jnp.broadcast_to(tile[i : i + 1], shape)
    done = []
    for b in range(n // 8):
        columns = [along_row(tiles[b], 8 * b + k) for k in range(8)]
        entry = [[spread(columns[k], i) if i >= k else None for k in range(8)] for i in range(8)]
        row = [spread(tiles[b], i) for i in range(8)]
        unit_row = [spread(units[b], i) for i in range(8)]
        inverse, factor = [None] * 8, [[None] * 8 for _ in range(8)]
        for k in range(8):
            inverse[k] = 1.0 / entry[k][k]
            for i in range(k + 1, 8):
                factor[i][k] = entry[i][k] * inverse[k]
                for j in range(k + 1, i + 1):
                    entry[i][j] = entry[i][j] - factor[i][k] * entry[j][k]
                row[i] = row[i] - factor[i][k] * row[k]
                unit_row[i] = unit_row[i] - factor[i][k] * unit_row[k]
        result = jnp.zeros(shape, F32)
        for k in range(8):
            result = jnp.where(sub == k, unit_row[k] * lax.rsqrt(entry[k][k]), result)
        done.append(result)
        for t in range(b + 1, n // 8):
            column = [along_row(tiles[t], 8 * b + k) for k in range(8)]
            for k in range(8):
                for m in range(k):
                    column[k] = column[k] - factor[k][m] * column[m]
                scaled = column[k] * inverse[k]
                tiles[t] = tiles[t] - scaled * row[k]
                units[t] = units[t] - scaled * unit_row[k]
    return jnp.concatenate(done, axis=0)


def basis_kernel(place, pieces_ref, start_ref, out_ref, gram_ref):
    count, size = pieces_ref.shape[0], pieces_ref.shape[1]
    for core in range(2):
        for chip in range(2):
            for d in range(4):
                at = (
                    lax.rem(place[1] + core, 2) * 8
                    + lax.rem(place[0] + chip, 2) * 4
                    + lax.bitwise_xor(place[2], d)
                )
                gram_ref[pl.ds(pl.multiple_of(at * size, 8), size), :] = pieces_ref[(core * 2 + chip) * 4 + d]
    half = gram_ref.shape[1]
    g00, g10, g11 = (gram_ref[i * half : (i + 1) * half, :] for i in range(3))
    g01 = g10.T
    dot = lambda a, b: jnp.dot(a, b, precision=HIGHEST, preferred_element_type=F32)
    out_ref[...] = start_ref[...]

    def iterate(_, carry):
        top, low = out_ref[:half], out_ref[half:]
        images = jnp.concatenate([dot(g00, top) + dot(g01, low), dot(g10, top) + dot(g11, low)], axis=0)
        small = dot(images.T, images)
        out_ref[...] = dot(images, inverse_factor(small).T)
        return carry

    lax.fori_loop(0, ITERS, iterate, 0)


def subspace(place, pieces, start):
    count, size, width = pieces.shape
    return call(
        "subspace_k",
        basis_kernel,
        (1,),
        [
            pl.BlockSpec(pieces.shape, lambda i, place: (0, 0, 0)),
            pl.BlockSpec(start.shape, lambda i, place: (0, 0)),
        ],
        pl.BlockSpec(start.shape, lambda i, place: (0, 0)),
        jax.ShapeDtypeStruct(start.shape, F32),
        [pltpu.VMEM((count * size, width), F32)],
        vmem=12,
    )(place, pieces, start)


def core_kernel(counts, steps, place, basis_ref, *rest):
    lines, (keep_ref, send_ref, factor_ref) = rest[: sum(counts)], rest[-3:]
    rank = basis_ref.shape[1]
    xs = basis_ref.shape[0] // 4

    @pl.when(pl.program_id(0) == 0)
    def _():
        for d in range(4):
            base = pl.multiple_of(lax.bitwise_xor(place[2], d) * xs, xs)
            high, low = split(basis_ref[pl.ds(base, xs), :])
            factor_ref[d * xs : (d + 1) * xs, 0:rank] = high
            factor_ref[d * xs : (d + 1) * xs, rank:] = low

    factor = factor_ref[...]

    def work(groups):
        lines = [
            jnp.concatenate([piece[r] for piece in pieces], axis=0) for pieces in groups for r in range(pieces[0].shape[0])
        ]
        high, low = split(jnp.concatenate(lines, axis=1))
        both = tn_dot(high, factor)
        out = both[:, :rank] + (both[:, rank:] + tn_dot(low, factor[:, :rank]))
        out = out.reshape(len(lines), 2, LANES // 2, rank)
        first = place[1] == 0
        keep_ref[0] = jnp.where(first, out[:, 0], out[:, 1])
        send_ref[...] = jnp.where(first, out[:, 1], out[:, 0])

    groups, at = [], 0
    for count in counts:
        groups.append(lines[at : at + count])
        at += count
    if steps is None:
        work(groups)
    else:
        for step, members in enumerate(steps):

            @pl.when(pl.program_id(0) == step)
            def _(members=members):
                work([groups[member] for member in members])


def core_of(place, basis, lines, species, whole):
    block = 8
    rank = basis.shape[1]
    groups = [[piece for d in group for piece in d] for group in lines]
    flat = [piece for group in groups for piece in group]
    rows = [group[0].shape[0] for group in groups]
    total, zs = sum(rows), flat[0].shape[2]
    before = [] if whole is None else [whole]
    if len(groups) == 1:
        steps = None
        specs = [pl.BlockSpec((block, *piece.shape[1:]), lambda i, place: (i, 0, 0)) for piece in flat]
    else:
        steps, at = [[] for _ in range(total // block)], 0
        for member, count in enumerate(rows):
            steps[at // block].append(member)
            at += count
        specs = [pl.BlockSpec(piece.shape, lambda i, place: (0, 0, 0)) for piece in flat]
    return call(
        "core_k",
        lambda place, *refs: core_kernel([len(group) for group in groups], steps, place, *refs),
        (total // block,),
        [pl.BlockSpec(basis.shape, lambda i, place: (0, 0))] + specs + [pl.BlockSpec(memory_space=pl.ANY)] * len(before),
        [
            pl.BlockSpec((1, block, zs // 2, rank), lambda i, place: (2 * place[1] + species, i, 0, 0)),
            pl.BlockSpec((block, zs // 2, rank), lambda i, place: (i, 0, 0)),
        ],
        [pltpu.HBM((4, total, zs // 2, rank), F32), pltpu.HBM((total, zs // 2, rank), F32)],
        [pltpu.VMEM((basis.shape[0], 2 * rank), BF16)],
        vmem=36,
        aliases={2 + len(flat): 0} if before else {},
    )(place, basis, *in_hbm(*flat, *before))


def finish_kernel(place, whole_ref, *refs):
    out_ref = refs[-1]
    for species, ref in enumerate(refs[:-1]):
        out_ref[species] = ref[...]


def finish(place, whole, came):
    rows, zs, rank = came[0].shape
    block = 8
    return call(
        "finish_k",
        finish_kernel,
        (rows // block,),
        [pl.BlockSpec(memory_space=pl.ANY)] + [pl.BlockSpec((block, zs, rank), lambda i, place: (i, 0, 0))] * 2,
        pl.BlockSpec((2, block, zs, rank), lambda i, place: (1 - place[1], i, 0, 0)),
        pltpu.HBM(whole.shape, F32),
        aliases={1: 0},
    )(place, *in_hbm(whole), *came)


def after(value, *earlier):
    return lax.optimization_barrier((value, *earlier))[0]


def pair_swap(value, distance):
    return lax.ppermute(value, "ba", [(i, i ^ distance) for i in range(4)])


def z_swap(value, d):
    return lax.ppermute(value, "aa", [(i, i ^ d) for i in range(4)])


def reduce_gram(place, gram):
    chip, core, z = place[0], place[1], place[2]
    rows, width = gram.shape
    halves = gram.reshape(2, rows // 2, width)
    take = lambda array, i: lax.dynamic_index_in_dim(array, i, 0, keepdims=False)
    gram = take(halves, core) + pair_swap(take(halves, 1 - core), 1)
    halves = gram.reshape(2, rows // 4, width)
    gram = take(halves, chip) + pair_swap(take(halves, 1 - chip), 2)
    blocks = gram.reshape(4, rows // 16, width)
    came = [z_swap(take(blocks, z ^ d), d) for d in (1, 2, 3)]
    gram = take(blocks, z) + came[0] + came[1] + came[2]
    gram = jnp.stack([gram] + [z_swap(gram, d) for d in (1, 2, 3)])
    gram = jnp.concatenate([gram, pair_swap(gram, 2)])
    return jnp.concatenate([gram, pair_swap(gram, 1)])


def fast_body(slab_field, x_basis, y_basis):
    rank = x_basis.shape[1]
    species, xs, ys, zs = slab_field.shape
    ba = lax.axis_index("ba")
    chip, core, z = ba // 2, ba % 2, lax.axis_index("aa")
    place = jnp.stack([chip, core, z]).astype(jnp.int32)
    rows = lambda index: lax.dynamic_slice_in_dim(y_basis, index * ys, ys, 0)
    basis_t = jnp.concatenate([rows(ba), rows(ba ^ 1)], axis=0).T

    share = rank // 4
    jobs, at = [], 0
    for size in X_PARTS:
        jobs.append((0, at, size, (share,)))
        at += size
    late = [(1, start, xs // 2, R_PARTS) for start in (0, xs // 2)]
    jobs[3:3] = late
    keeps, sends, came, lines = [], [], [], []
    halves = []
    grams = [jnp.zeros((len(PAIRS) * xs * 2, xs * 2), F32)]
    count = len(X_PARTS)

    def spread(i):
        mine = add_up(place, keeps[i], came[i])
        line = [mine[0], None, None, None]
        for d, earlier in ((2, 1), (3, 2), (1, 3)):
            ready = [lines[-1][earlier]] if lines else []
            if i + 1 == len(X_PARTS) + len(R_PARTS) and d == 1:
                ready.append(grams[-2])
            part = after(mine[d], *ready)
            line[d] = z_swap(part, d)
        lines.append(line)
        if i >= count - 1:
            group = [[old[d] for old in lines[:count]] for d in range(4)] if i == count - 1 else [[part] for part in line]
            grams.append(add_gram(place, grams[-1], group))

    def exchange(part):
        i = len(came)
        earlier = []
        if i >= 2:
            earlier = [came[i - 2]] + (lines[i - 3][2:3] if i >= 3 else []) + (lines[i - 4][1:] if i >= 4 else [])
        if i in (6, 7):
            earlier.append(halves[i - 6])
        if i >= count + 3:
            earlier.append(grams[i - count - 2])
        came.append(pair_swap(after(part, *earlier), 2))
        if i >= 1:
            spread(i - 1)

    swaps = [(0, 0, X_PARTS[0]), (0, X_PARTS[0], xs - X_PARTS[0]), (1, 0, xs)]
    others, theirs, second = [], [], []
    for job in jobs:
        while swaps and swaps[0][0] <= job[0] and swaps[0][1] <= job[1]:
            s, start, size = swaps.pop(0)
            earlier = ([], sends[:1], lines[0][:1] if lines else [])[len(theirs)]
            first = after(2 * (1 - core) + s, *earlier)
            theirs.append(lax.dynamic_slice(slab_field, (first, start, 0, 0), (1, size, ys, zs))[0])
            others.append((s, start, pair_swap(theirs[-1], 1)))
        base, other = [(start, array) for s, start, array in others if s == job[0] and start <= job[1]][-1]
        if job[0] == 0:
            keep, send = project(place, slab_field, other, basis_t, job, job[1] - base, job[2], [])
        else:
            keep, send = project(place, slab_field, other, basis_t, job, job[1] - base, xs, second)
            second = [*keep, *send]
            halves.append(send[0])
            continue
        for mine, part in zip(keep, send):
            keeps.append(mine)
            sends.append(part)
            exchange(part)
    for mine, part in zip(second[: len(R_PARTS)], second[len(R_PARTS) :]):
        keeps.append(mine)
        sends.append(part)
        exchange(part)
    spread(len(keeps) - 1)

    first = [[line[d] for line in lines[:count]] for d in range(4)]
    second = [[[line[d]] for d in range(4)] for line in lines[count:]]
    basis = subspace(place, reduce_gram(place, grams[-1]), x_basis)

    whole, send0 = core_of(place, basis, [first], 0, None)
    came0 = pair_swap(send0, 1)
    whole, send1 = core_of(place, basis, second, 1, whole)
    core_tensor = finish(place, whole, [came0, pair_swap(send1, 1)]).transpose(0, 3, 1, 2)
    new_basis = lax.dynamic_slice_in_dim(basis, z * xs, xs, 0)
    return new_basis, core_tensor


def orthonormal(images):
    small = jnp.dot(images.T, images, precision=HIGHEST)
    lower = jnp.linalg.cholesky(small)
    return lax.linalg.triangular_solve(lower, images, left_side=False, lower=True, transpose_a=True)


def plain_body(slab_field, x_basis, y_basis):
    y_rows = slab_field.shape[2]
    local_basis = lax.dynamic_slice_in_dim(y_basis, lax.axis_index("ba") * y_rows, y_rows, 0)
    partial_value = jnp.einsum("sxyz,yr->sxrz", slab_field, local_basis, precision=HIGHEST)
    projected = lax.psum_scatter(partial_value, "ba", scatter_dimension=3, tiled=True)
    columns = lax.all_to_all(projected, "aa", split_axis=2, concat_axis=1, tiled=True)
    basis = x_basis
    local_gram = jnp.einsum("sxrz,svrz->xv", columns, columns, precision=HIGHEST)
    gram_matrix = lax.psum(local_gram, ("aa", "ba"))
    for _ in range(ITERS):
        basis = orthonormal(jnp.dot(gram_matrix, basis, precision=HIGHEST))
    core_tensor = jnp.einsum("xk,sxrz->skrz", basis, columns, precision=HIGHEST)
    basis_rows = x_basis.shape[0] // lax.axis_size("aa")
    new_basis = lax.dynamic_slice_in_dim(basis, lax.axis_index("aa") * basis_rows, basis_rows, 0)
    return new_basis, core_tensor


def solution(mesh):
    def body(slab_field, x_basis, y_basis):
        fits = (
            mesh.shape["aa"] == 4
            and mesh.shape["ba"] == 4
            and slab_field.shape == (4, LANES, LANES, 2 * LANES)
            and x_basis.shape == y_basis.shape == (4 * LANES, LANES)
        )
        return (fast_body if fits else plain_body)(slab_field, x_basis, y_basis)

    return jax.shard_map(
        body,
        mesh=mesh,
        in_specs=(P("slab", "aa", "ba", None), P("slab", None), P("slab", None)),
        out_specs=(P(("slab", "aa"), None), P("slab", None, "aa", "ba")),
        check_vma=False,
    )
```
